128 devices in a mesh: pulse: 8 (over y, core), tile: 16 (over z, x).
Axes of the slice: x: 4, y: 4, z: 4, core: 2. Of those that a mesh axis runs over, the one named last changes fastest.
Arguments:
- echoes: bfloat16 [65536, 2, 4096], P(('pulse', 'tile')), may hold values from -6 to 6
- phases: float32 [65536], P(('pulse', 'tile')), may hold values from -3.140625 to 3.140625
- kernel: bfloat16 [128, 256, 256], P(('pulse', 'tile')), may hold values from -0.375 to 0.375
- steering: bfloat16 [128, 12, 256, 1024], P(('pulse', 'tile')), may hold values from -0.0546875 to 0.0546875
- footprint: int32 [128, 12], P(('pulse', 'tile')), may hold values from 0 to 31, as said below
- counts: int32 [128], P(('pulse', 'tile')), may hold values from 1 to 12, as said below
- range_start: int32 [128, 2], P(('pulse', 'tile')), may hold values from 0 to 3840
Outputs:
- scene_tiles: float32 [2, 16, 256, 512], P(None, 'tile', 'pulse')
- phase_grad: float32 [65536], P(('pulse', 'tile'))
The draws below stay inside these ranges and needn't reach their ends.
Inputs may be any that keep to these rules, and one draw needn't show every extreme that they name: `footprint`: only the first counts[b] entries of block b's list are used. The used entries of one block name tiles of distinct columns (id modulo 16). Some tile column is named by the used entries of every block. Some block uses all 12 entries. `counts`: some block has exactly 12.
All inputs are finite; a program needn't handle non-finite values.
Results may differ from the reference program's by a relative error of at most 0.0071.
Values may be sent and summed in bfloat16 or wider, within the bound.
A program may use at most 128 MiB of HBM per device.

```python
import math
import jax
import jax.numpy as jnp
from jax import lax

PB = 512
NS = 4096
WIN = 256
R = 256
C = 256
TROWS = 2
F = 12
PULSES = 65536
N_TILE = 16
DEVICES = 128


def plan_tiles(key):
    key_count, key_owner, key_perm, key_spot, key_row, key_force = jax.random.split(key, 6)
    raw_draw = jax.random.randint(key_count, (DEVICES,), 0, 64)
    counts = 1 + (F - 1) * raw_draw * raw_draw // (63 * 63)
    forced = jax.random.randint(key_force, (), 0, DEVICES)
    device_index = jnp.arange(DEVICES, dtype=jnp.int32)
    counts = jnp.where(device_index == forced, F, counts).astype(jnp.int32)
    shared_col = jax.random.randint(key_owner, (), 0, N_TILE)
    orders = jax.vmap(lambda sub: jax.random.permutation(sub, N_TILE))(jax.random.split(key_perm, DEVICES)).astype(jnp.int32)
    position = jnp.argmax(orders == shared_col, axis=1).astype(jnp.int32)
    target = (jax.random.randint(key_spot, (DEVICES,), 0, 1 << 20) % counts).astype(jnp.int32)
    column_index = jnp.arange(N_TILE, dtype=jnp.int32)[None, :]
    at_target = jnp.take_along_axis(orders, target[:, None], axis=1)
    orders = jnp.where(column_index == position[:, None], at_target, orders)
    orders = jnp.where(column_index == target[:, None], shared_col, orders)
    tile_rows = jax.random.randint(key_row, (DEVICES, F), 0, TROWS)
    footprint = (tile_rows * N_TILE + orders[:, :F]).astype(jnp.int32)
    return (footprint, counts)


def draw_footprint(key, part):
    return plan_tiles(key)[0]


def draw_counts(key, part):
    return plan_tiles(key)[1]


def plant(entries, rng, low, largest):
    extent = entries.shape
    place = [jax.random.randint(jax.random.fold_in(rng, axis), (), 0, extent[axis]) for axis in range(len(extent))]
    entries = entries.at[tuple(place)].set(low)
    longest = extent.index(max(extent))
    place[longest] = (place[longest] + 1) % extent[longest]
    return entries.at[tuple(place)].set(largest)


def level_of(key, extent, pieces, low, top_value):
    level = 1.0
    for dim, parts in pieces:
        steps = jax.random.uniform(jax.random.fold_in(jax.random.fold_in(key, 6), dim), (parts,), jnp.float32, low / len(pieces), top_value / len(pieces))
        level = level * jnp.repeat(jnp.exp(steps), extent[dim] // parts).reshape((-1,) + (1,) * (len(extent) - 1 - dim))
    return level


def gaussian(stream_key, shape, deviation, limit, shards=(), kind=jnp.bfloat16):
    array = jax.random.normal(stream_key, shape, jnp.float32) * deviation
    if len(shards) > 0:
        array = level_of(stream_key, shape, shards, -0.22, 0.18) * array
    return jnp.clip(array, min=-limit, max=limit).astype(kind)


def setup_inputs(seed: int = 0) -> dict:
    splits = jax.random.split(jax.random.key(seed), 8)
    return {
        "echoes": gaussian(splits[0], (PULSES, 2, NS), 1.0, 6.0, ((0, 128),)),
        "phases": jnp.clip(jax.random.uniform(splits[1], (PULSES,), jnp.float32, -3.140625, 3.140625), -3.140625, 3.140625),
        "kernel": gaussian(splits[2], (DEVICES, WIN, C), WIN ** -0.5, 0.375, ((0, 128),)),
        "steering": gaussian(splits[3], (DEVICES, F, R, 2 * PB), (2 * PB * F) ** -0.5, 0.0546875, ((0, 128),)),
        "footprint": draw_footprint(jax.random.fold_in(splits[7], 71), 0),
        "counts": draw_counts(jax.random.fold_in(splits[7], 71), 0),
        "range_start": plant(jax.random.randint(splits[6], (DEVICES, TROWS), 0, NS - WIN + 1), jax.random.fold_in(splits[6], 1), 0, NS - WIN).astype(jnp.int32),
    }


def phased(steer_slot, cosine, sines):
    real_part = steer_slot[:, :PB].astype(jnp.float32)
    imag_part = steer_slot[:, PB:].astype(jnp.float32)
    turned_re = real_part * cosine[None, :] - imag_part * sines[None, :]
    turned_im = real_part * sines[None, :] + imag_part * cosine[None, :]
    return jnp.concatenate([turned_re, turned_im], axis=1).astype(jnp.bfloat16)

def window_product(pulse_block, interp, start):
    window = lax.dynamic_slice_in_dim(pulse_block, start, WIN, 2).reshape(2 * PB, WIN)
    return jnp.dot(window, interp, preferred_element_type=jnp.float32).astype(jnp.bfloat16).reshape(PB, 2 * C)

def tile_part(steer_ph, profile):
    real_part = profile[:, :C]
    imag_part = profile[:, C:]
    stacked = jnp.concatenate([profile, jnp.concatenate([-imag_part, real_part], axis=1)], axis=0)
    return jnp.dot(steer_ph, stacked, preferred_element_type=jnp.float32)

def reference(echoes, phases, kernel, steering, footprint, counts, range_start):
    anchor = jnp.zeros((), jnp.int32)

    def add_device(device, scene):
        device = device.astype(jnp.int32)
        pulse_block = lax.dynamic_slice_in_dim(echoes, device * PB, PB, 0)
        phase_block = lax.dynamic_slice_in_dim(phases, device * PB, PB, 0)
        cosine = jnp.cos(phase_block)
        sines = jnp.sin(phase_block)

        def add_slot(slot, accum):
            tile_id = footprint[device, slot]
            tile_row = (tile_id // N_TILE).astype(jnp.int32)
            column = (tile_id % N_TILE).astype(jnp.int32)
            profile = window_product(pulse_block, kernel[device], range_start[device, tile_row])
            partial_value = tile_part(phased(steering[device, slot], cosine, sines), profile)
            current = lax.dynamic_slice(accum, (tile_row, column, anchor, anchor), (1, 1, R, 2 * C))
            return lax.dynamic_update_slice(accum, current + partial_value[None, None], (tile_row, column, anchor, anchor))
        return lax.fori_loop(jnp.int32(0), counts[device], add_slot, scene)
    scene_tiles = lax.fori_loop(jnp.int32(0), jnp.int32(DEVICES), add_device, jnp.zeros((TROWS, N_TILE, R, 2 * C), jnp.float32))
    power = scene_tiles[..., :C] ** 2 + scene_tiles[..., C:] ** 2
    weight = (scene_tiles * jnp.concatenate([power, power], axis=-1)).astype(jnp.bfloat16)
    factor = -4.0 / math.sqrt(R * C)

    def device_grad(device):
        device = device.astype(jnp.int32)
        pulse_block = lax.dynamic_slice_in_dim(echoes, device * PB, PB, 0)
        phase_block = lax.dynamic_slice_in_dim(phases, device * PB, PB, 0)
        cosine = jnp.cos(phase_block)
        sines = jnp.sin(phase_block)

        def add_slot(slot, gradient):
            tile_id = footprint[device, slot]
            tile_row = (tile_id // N_TILE).astype(jnp.int32)
            column = (tile_id % N_TILE).astype(jnp.int32)
            profile = window_product(pulse_block, kernel[device], range_start[device, tile_row])
            steer_ph = phased(steering[device, slot], cosine, sines).astype(jnp.float32)
            weight_tile = weight[tile_row, column]
            paired = jnp.concatenate([profile, jnp.concatenate([profile[:, C:], -profile[:, :C]], axis=1)], axis=0)
            moments = lax.dot_general(weight_tile, paired, (((1,), (1,)), ((), ())), preferred_element_type=jnp.float32)
            term = steer_ph[:, :PB] * moments[:, PB:] + steer_ph[:, PB:] * moments[:, :PB]
            return gradient + lax.optimization_barrier(jnp.sum(term, axis=0))
        gradient = lax.fori_loop(jnp.int32(0), counts[device], add_slot, jnp.zeros((PB,), jnp.float32))
        return gradient * factor
    gradients = lax.map(device_grad, jnp.arange(DEVICES, dtype=jnp.int32))
    return (scene_tiles, gradients.reshape(PULSES))
```

```python
import functools
import math

import jax
import jax.numpy as jnp
from jax import lax
from jax.experimental import pallas as pl
from jax.experimental.pallas import tpu as pltpu
from jax.sharding import PartitionSpec as P

MESH = pl.DeviceIdType.MESH
SIDE = 4
LANE = 128
SUB = 16
PARTS = (
    (0, 5, (0, 1, 2)),
    (5, 10, (1, 2, 0)),
    (10, 16, (2, 0, 1)),
)


def position():
    p = lax.axis_index("pulse")
    t = lax.axis_index("tile")
    return (p // 2, t // SIDE, t % SIDE), p % 2


def device_at(where, core):
    return (where[0] * 2 + core, where[1] * SIDE + where[2])


def shifted(where, axis, d):
    moved = list(where)
    moved[axis] = lax.rem(where[axis] + d, SIDE)
    return tuple(moved)


def pick(fixed, lo, hi):
    return tuple(fixed.get(a, slice(None)) for a in range(3)) + (slice(lo, hi),)


def main_kernel(
    plan_ref,
    mask_in,
    trig_in,
    stacked_in,
    paired_in,
    steer_in,
    scene_ref,
    grad_ref,
    mask,
    omask,
    trig,
    stacked,
    paired,
    steer,
    tiles,
    crecv,
    s1,
    r1a, r1b, r1c,
    s2a, s2b, s2c,
    r2a, r2b, r2c,
    s3a, s3b, s3c,
    r3a, r3b, r3c,
    units,
    wf,
    acc,
    lsem,
    msem,
    csend, crcv,
    s1send, s1recv,
    s2send, s2recv,
    s3send, s3recv,
    gsend, grecv,
    fsend, frecv,
):
    r1, s2, r2, s3, r3 = (r1a, r1b, r1c), (s2a, s2b, s2c), (r2a, r2b, r2c), (s3a, s3b, s3c), (r3a, r3b, r3c)
    where, core = position()
    other = device_at(where, 1 - core)
    pulses = trig.shape[1]
    slots = steer.shape[0]

    local = []
    for n, (src, dst) in enumerate(
        ((mask_in, mask), (trig_in, trig), (stacked_in, stacked), (paired_in, paired))
    ):
        cp = pltpu.make_async_copy(src, dst, lsem.at[slots + n])
        cp.start()
        local.append(cp)
    for j in range(slots):
        pltpu.make_async_copy(steer_in.at[j], steer.at[j], lsem.at[j]).start()

    barrier = pltpu.get_barrier_semaphore()
    pl.semaphore_signal(barrier, inc=1, device_id=other, device_id_type=MESH)
    for axis in range(3):
        for d in range(1, SIDE):
            pl.semaphore_signal(
                barrier, inc=1, device_id=device_at(shifted(where, axis, d), core), device_id_type=MESH
            )
    local[0].wait()
    local[1].wait()

    def turn(j, carry):
        pltpu.make_async_copy(steer_in.at[j], steer.at[j], lsem.at[j]).wait()
        cosine = trig[0:1, :]
        sines = trig[1:2, :]

        def rows(i, c2):
            at = pl.ds(pl.multiple_of(i * 64, 64), 64)
            re = steer[j, at, :pulses].astype(jnp.float32)
            im = steer[j, at, pulses:].astype(jnp.float32)
            steer[j, at, :pulses] = (re * cosine - im * sines).astype(jnp.bfloat16)
            steer[j, at, pulses:] = (re * sines + im * cosine).astype(jnp.bfloat16)
            return c2

        return lax.fori_loop(0, steer.shape[1] // 64, rows, carry)

    lax.fori_loop(0, slots, turn, 0)

    pl.semaphore_wait(barrier, 10)
    mcopy = pltpu.make_async_remote_copy(
        src_ref=mask, dst_ref=omask, send_sem=msem.at[0], recv_sem=msem.at[1], device_id=other, device_id_type=MESH
    )
    mcopy.start()
    local[2].wait()
    local[3].wait()

    def core_copy(t):
        return pltpu.make_async_remote_copy(
            src_ref=tiles.at[t, :, 1 - core],
            dst_ref=crecv.at[t],
            send_sem=csend.at[t],
            recv_sem=crcv.at[t],
            device_id=other,
            device_id_type=MESH,
        )

    stage1 = []

    def send1(p, d, sub, src_fixed, sem):
        lo, hi, order = PARTS[p]
        axis = order[0]
        fixed = dict(src_fixed)
        target = shifted(where, axis, d)
        fixed[axis] = target[axis]
        rest = tuple(a for a in range(3) if a != axis)
        dst = tuple(src_fixed.get(a, slice(None)) for a in rest)
        cp = pltpu.make_async_remote_copy(
            src_ref=s1.at[pick(fixed, lo, hi)],
            dst_ref=r1[p].at[(d - 1,) + dst],
            send_sem=s1send.at[sem],
            recv_sem=s1recv.at[sem],
            device_id=device_at(target, core),
            device_id_type=MESH,
        )
        cp.start()
        return cp

    for g in range(SIDE):
        z = lax.rem(where[1] + 1 + g, SIDE)

        def compute(x, carry):
            t = z * SIDE + x
            left = steer[plan_ref[0, t]]
            right = stacked[plan_ref[1, t]]
            part = jnp.dot(left, right, preferred_element_type=jnp.float32)
            tiles[t] = part.reshape(tiles.shape[1:])
            core_copy(t).start()
            return carry

        lax.fori_loop(0, SIDE, compute, 0)
        if g == 0:
            mcopy.wait()

        def combine(x, carry):
            t = z * SIDE + x
            core_copy(t).wait_recv()
            for k in range(2):
                m = mask[pl.ds(t * 2 + k, 1), :]
                om = omask[pl.ds(t * 2 + k, 1), :]
                for lg in range(4):
                    lanes = slice(lg * LANE, (lg + 1) * LANE)
                    for y in range(SIDE):
                        v = tiles[t, y, core, :, lanes] * m + crecv[t, y, :, lanes] * om
                        u = k * 8 + lg * 2
                        s1[y, z, x, u : u + 2] = v.astype(jnp.bfloat16).reshape(2, SUB, LANE)
            return carry

        lax.fori_loop(0, SIDE, combine, 0)
        for d in range(1, SIDE):
            stage1.append(send1(0, d, g, {1: z}, g * 6 + d - 1))
            stage1.append(send1(2, d, g, {1: z}, g * 6 + 3 + d - 1))
        if g < SIDE - 1:
            stage1.append(send1(1, g + 1, 0, {}, 24 + g))

    def all_core(t, carry):
        core_copy(t).wait_send()
        return carry

    for cp in stage1:
        cp.wait_recv()

    stage2 = []
    for p, (lo, hi, order) in enumerate(PARTS):
        a, b, _ = order
        rest = [x for x in range(3) if x != a]
        bpos = rest.index(b)

        def add(i, carry):
            o = lax.rem(i, SIDE)
            q = i // SIDE
            fixed = {a: where[a], rest[0]: q, rest[1]: o}
            v = s1[pick(fixed, lo, hi)].astype(jnp.float32)
            for d in range(SIDE - 1):
                v = v + r1[p][d, q, o].astype(jnp.float32)
            s2[p][q, o] = v
            return carry

        lax.fori_loop(0, SIDE * SIDE, add, 0)
        for d in range(1, SIDE):
            target = shifted(where, b, d)
            idx = (target[b],) if bpos == 0 else (slice(None), target[b])
            cp = pltpu.make_async_remote_copy(
                src_ref=s2[p].at[idx],
                dst_ref=r2[p].at[d - 1],
                send_sem=s2send.at[p * 3 + d - 1],
                recv_sem=s2recv.at[p * 3 + d - 1],
                device_id=device_at(target, core),
                device_id_type=MESH,
            )
            cp.start()
            stage2.append(cp)

    stage3 = []
    for p, (lo, hi, order) in enumerate(PARTS):
        a, b, c = order
        rest = [x for x in range(3) if x != a]
        bpos = rest.index(b)
        for cp in stage2[p * 3 : p * 3 + 3]:
            cp.wait_recv()
        for q in range(SIDE):
            v = s2[p][where[b], q] if bpos == 0 else s2[p][q, where[b]]
            for d in range(SIDE - 1):
                v = v + r2[p][d, q]
            s3[p][q] = v
        for d in range(1, SIDE):
            target = shifted(where, c, d)
            cp = pltpu.make_async_remote_copy(
                src_ref=s3[p].at[target[c]],
                dst_ref=r3[p].at[d - 1],
                send_sem=s3send.at[p * 3 + d - 1],
                recv_sem=s3recv.at[p * 3 + d - 1],
                device_id=device_at(target, core),
                device_id_type=MESH,
            )
            cp.start()
            stage3.append(cp)

    for p, (lo, hi, order) in enumerate(PARTS):
        for cp in stage3[p * 3 : p * 3 + 3]:
            cp.wait_recv()
        v = s3[p][where[order[2]]]
        for d in range(SIDE - 1):
            v = v + r3[p][d]
        units[lo:hi] = v

    y0, z0, x0 = where
    for k in range(2):
        for lg in range(2):
            for rh in range(2):
                ur = k * 8 + lg * 2 + rh
                re = units[ur]
                im = units[ur + 4]
                power = re * re + im * im
                wf[core, y0, z0, x0, ur] = (re * power).astype(jnp.bfloat16)
                wf[core, y0, z0, x0, ur + 4] = (im * power).astype(jnp.bfloat16)
                rows = slice(rh * SUB, (rh + 1) * SUB)
                scene_ref[k, rows, lg * LANE : (lg + 1) * LANE] = re
                scene_ref[k, rows, (lg + 2) * LANE : (lg + 3) * LANE] = im

    done = []

    def gather(p, step):
        lo, hi, order = PARTS[p]
        axis = order[2 - step]
        keep = order[: 3 - step]
        fixed = {a: where[a] for a in keep}
        src = wf.at[(core,) + pick(fixed, lo, hi)]
        out = []
        for d in range(1, SIDE):
            n = (step * 3 + p) * 3 + d - 1
            cp = pltpu.make_async_remote_copy(
                src_ref=src,
                dst_ref=src,
                send_sem=gsend.at[n],
                recv_sem=grecv.at[n],
                device_id=device_at(shifted(where, axis, d), core),
                device_id_type=MESH,
            )
            cp.start()
            out.append(cp)
        return out

    def forward(p, step, d):
        lo, hi, order = PARTS[p]
        axis = order[2 - step]
        keep = order[: 3 - step]
        fixed = {a: where[a] for a in keep}
        fixed[axis] = lax.rem(where[axis] + SIDE - d, SIDE)
        src = wf.at[(core,) + pick(fixed, lo, hi)]
        n = (step * 3 + p) * 4 + d
        cp = pltpu.make_async_remote_copy(
            src_ref=src,
            dst_ref=src,
            send_sem=fsend.at[n],
            recv_sem=frecv.at[n],
            device_id=other,
            device_id_type=MESH,
        )
        cp.start()
        return cp

    gathers = {}
    forwards = []
    for p in range(3):
        gathers[p] = gather(p, 0)
        forwards.append(forward(p, 0, 0))
    for step in range(3):
        for p in range(3):
            current = gathers[p]
            for d in range(1, SIDE):
                current[d - 1].wait_recv()
                forwards.append(forward(p, step, d))
            done.extend(current)
            if step < 2:
                gathers[p] = gather(p, step + 1)
    for cp in forwards:
        cp.wait_recv()

    acc[...] = jnp.zeros_like(acc)

    def backward(j, carry):
        zj = plan_ref[2, j]
        xj = plan_ref[3, j]
        kj = plan_ref[4, j]
        live = jnp.where(plan_ref[5, j] > 0, jnp.float32(1.0), jnp.float32(0.0))
        groups = []
        for lg in range(4):
            pieces = [
                wf[c, y, zj, xj, pl.ds(kj * 8 + lg * 2, 2)].reshape(2 * SUB, LANE)
                for y in range(SIDE)
                for c in range(2)
            ]
            groups.append(jnp.concatenate(pieces, axis=0))
        weight = jnp.concatenate(groups, axis=1)
        moments = lax.dot_general(
            weight, paired[kj], (((1,), (1,)), ((), ())), preferred_element_type=jnp.float32
        )
        re = steer[j, :, :pulses].astype(jnp.float32)
        im = steer[j, :, pulses:].astype(jnp.float32)
        term = re * moments[:, pulses:] + im * moments[:, :pulses]
        acc[...] += jnp.sum(term.reshape(-1, 8, pulses), axis=0) * live
        return carry

    lax.fori_loop(0, slots, backward, 0)
    factor = -4.0 / math.sqrt(steer.shape[1] * (stacked.shape[2] // 2))
    grad_ref[...] = jnp.sum(acc[...], axis=0, keepdims=True) * factor

    lax.fori_loop(0, 4 * SIDE, all_core, 0)
    for cp in stage1 + stage2 + stage3 + done + forwards:
        cp.wait_send()


def on_device(echoes, phases, kernel, steering, footprint, counts, range_start):
    columns = lax.axis_size("tile")
    row_parts = lax.axis_size("pulse")
    pulses = echoes.shape[0]
    window_len = kernel.shape[1]
    breadth = kernel.shape[2]
    height = steering.shape[2]
    slots = steering.shape[1]
    tile_rows = range_start.shape[1]
    part_rows = height // row_parts
    width = 2 * breadth
    ids = footprint[0]
    used = jnp.arange(slots, dtype=jnp.int32) < counts[0]
    hit = (ids[None, :] % columns == jnp.arange(columns, dtype=jnp.int32)[:, None]) & used[None, :]
    slot_of = jnp.sum(jnp.where(hit, jnp.arange(slots, dtype=jnp.int32)[None, :], 0), axis=1)
    label = jnp.sum(jnp.where(hit, ids[None, :] // columns + 1, 0), axis=1) - 1
    pad = lambda v: jnp.pad(v, (0, columns - slots))
    plan = jnp.stack(
        [
            slot_of,
            jnp.maximum(label, 0),
            pad(ids % columns // SIDE),
            pad(ids % SIDE),
            pad(ids // columns),
            pad(used.astype(jnp.int32)),
        ]
    )
    mask = (label[:, None] == jnp.arange(tile_rows)[None, :]).astype(jnp.float32).reshape(-1, 1)
    mask = jnp.broadcast_to(mask, (columns * tile_rows, LANE))
    trig = jnp.stack([jnp.cos(phases), jnp.sin(phases)])
    stacked, paired = [], []
    for k in range(tile_rows):
        window = lax.dynamic_slice_in_dim(echoes, range_start[0, k], window_len, 2)
        prof = (
            jnp.dot(window.reshape(2 * pulses, window_len), kernel[0], preferred_element_type=jnp.float32)
            .astype(jnp.bfloat16)
            .reshape(pulses, width)
        )
        re, im = prof[:, :breadth], prof[:, breadth:]
        stacked.append(jnp.concatenate([prof, jnp.concatenate([-im, re], axis=1)], axis=0))
        paired.append(jnp.concatenate([prof, jnp.concatenate([im, -re], axis=1)], axis=0))
    stacked, paired = jnp.stack(stacked), jnp.stack(paired)

    f32, bf16 = jnp.float32, jnp.bfloat16
    sizes = [hi - lo for lo, hi, _ in PARTS]
    vmem = pltpu.VMEM
    sem = lambda n: pltpu.SemaphoreType.DMA((n,))
    anywhere = pl.BlockSpec(memory_space=pl.ANY)
    scene, grad = pl.pallas_call(
        main_kernel,
        out_shape=(
            jax.ShapeDtypeStruct((tile_rows, part_rows, width), f32),
            jax.ShapeDtypeStruct((1, pulses), f32),
        ),
        in_specs=[pl.BlockSpec(memory_space=pltpu.SMEM)] + [anywhere] * 5,
        out_specs=[pl.BlockSpec(memory_space=pltpu.VMEM)] * 2,
        scratch_shapes=[
            vmem(mask.shape, f32),
            vmem(mask.shape, f32),
            vmem(trig.shape, f32),
            vmem(stacked.shape, bf16),
            vmem(paired.shape, bf16),
            vmem((slots, height, 2 * pulses), bf16),
            vmem((columns, SIDE, 2, part_rows, width), f32),
            vmem((columns, SIDE, part_rows, width), f32),
            vmem((SIDE, SIDE, SIDE, 16, SUB, LANE), bf16),
        ]
        + [vmem((3, SIDE, SIDE, n, SUB, LANE), bf16) for n in sizes]
        + [vmem((SIDE, SIDE, n, SUB, LANE), f32) for n in sizes]
        + [vmem((3, SIDE, n, SUB, LANE), f32) for n in sizes]
        + [vmem((SIDE, n, SUB, LANE), f32) for n in sizes]
        + [vmem((3, n, SUB, LANE), f32) for n in sizes]
        + [
            vmem((16, SUB, LANE), f32),
            vmem((2, SIDE, SIDE, SIDE, 16, SUB, LANE), bf16),
            vmem((8, pulses), f32),
            sem(slots + 4),
            sem(2),
            sem(columns), sem(columns),
            sem(27), sem(27),
            sem(9), sem(9),
            sem(9), sem(9),
            sem(27), sem(27),
            sem(36), sem(36),
        ],
        compiler_params=pltpu.CompilerParams(
            collective_id=0, has_side_effects=True, vmem_limit_bytes=60 << 20
        ),
    )(plan, mask, trig, stacked, paired, steering[0])
    return (scene[:, None], grad[0])


def solution(mesh):
    placed = (
        P(("pulse", "tile"), None, None),
        P(("pulse", "tile")),
        P(("pulse", "tile"), None, None),
        P(("pulse", "tile"), None, None, None),
        P(("pulse", "tile"), None),
        P(("pulse", "tile")),
        P(("pulse", "tile"), None),
    )
    return jax.shard_map(
        on_device,
        mesh=mesh,
        in_specs=placed,
        out_specs=(P(None, "tile", "pulse", None), P(("pulse", "tile"))),
        check_vma=False,
    )
```

```python
import functools
import math

import jax
import jax.numpy as jnp
from jax import lax
from jax.experimental import pallas as pl
from jax.experimental.pallas import tpu as pltpu
from jax.sharding import PartitionSpec as P

MESH = pl.DeviceIdType.MESH
SIDE = 4
LANE = 128
SUB = 16
PARTS = (
    (0, 6, (0, 1, 2)),
    (6, 10, (1, 2, 0)),
    (10, 16, (2, 1, 0)),
)
NEAR_FIRST = (1, 3, 2)


def position():
    p = lax.axis_index("pulse")
    t = lax.axis_index("tile")
    core = p % 2
    return turned((p // 2, t // SIDE, t % SIDE), core), core


def turned(place, core):
    first = jnp.where(core == 0, place[0], place[2])
    last = jnp.where(core == 0, place[2], place[0])
    return (first, place[1], last)


def device_at(where, core):
    y, z, x = turned(where, core)
    return (y * 2 + core, z * SIDE + x)


def shifted(where, axis, d):
    moved = list(where)
    moved[axis] = lax.rem(where[axis] + d, SIDE)
    return tuple(moved)


def pick(fixed, lo, hi):
    return tuple(fixed.get(a, slice(None)) for a in range(3)) + (slice(lo, hi),)


def local_kernel(
    foot_ref,
    count_ref,
    start_ref,
    phases_ref,
    kernel_ref,
    echoes_in,
    plan_ref,
    mask,
    trig,
    stacked,
    windows,
    raw,
    sem,
):
    pulses = phases_ref.shape[1]
    window_len, breadth = kernel_ref.shape
    span = window_len + LANE
    last = (echoes_in.shape[2] - span) // LANE
    slots = foot_ref.shape[1]
    blocks = [jnp.minimum(start_ref[0, k] // LANE, last) for k in range(2)]
    copies = []
    for k in range(2):
        cp = pltpu.make_async_copy(
            echoes_in.at[:, :, pl.ds(pl.multiple_of(blocks[k] * LANE, LANE), span)], windows.at[k], sem.at[k]
        )
        cp.start()
        copies.append(cp)
    count = count_ref[0]
    for t in range(SIDE * SIDE):
        for n in range(6):
            plan_ref[n, t] = jnp.int32(0)
    tile_id = lax.broadcasted_iota(jnp.int32, mask.shape, 0)
    tile_id = tile_id // 2 + tile_id % 2 * (SIDE * SIDE)
    found = jnp.zeros(mask.shape, jnp.float32)
    for j in range(slots):
        name = foot_ref[0, j]
        live = j < count
        found = jnp.where(tile_id == jnp.where(live, name, -1), jnp.float32(1.0), found)
        plan_ref[2, j] = name // SIDE % SIDE
        plan_ref[3, j] = name % SIDE
        plan_ref[4, j] = name // (SIDE * SIDE)
        plan_ref[5, j] = live.astype(jnp.int32)

        @pl.when(live)
        def _():
            t = name % (SIDE * SIDE)
            plan_ref[0, t] = jnp.int32(j)
            plan_ref[1, t] = name // (SIDE * SIDE)

    mask[...] = found
    angle = phases_ref[...]
    trig[0:1, :] = jnp.cos(angle)
    trig[1:2, :] = jnp.sin(angle)
    depth = pulses // SIDE
    for k in range(2):
        weights = jnp.concatenate(
            [kernel_ref[...].astype(jnp.float32), jnp.zeros((LANE, breadth), jnp.float32)], axis=0
        )
        weights = pltpu.roll(weights, start_ref[0, k] - blocks[k] * LANE, 0).astype(jnp.bfloat16)
        copies[k].wait()

        def interpolate(i, carry):
            at = pl.multiple_of(i * depth, depth)
            window = windows[k, pl.ds(at, depth)]
            value = jnp.dot(window.reshape(2 * depth, span), weights, preferred_element_type=jnp.float32)
            top, low = pl.ds(at, depth), pl.ds(pulses + at, depth)
            for h in range(breadth // LANE):
                raw[h] = value[:, h * LANE : (h + 1) * LANE]
                re = raw[h, pl.ds(0, depth, stride=2), :].astype(jnp.bfloat16)
                im = raw[h, pl.ds(1, depth, stride=2), :].astype(jnp.bfloat16)
                left = slice(h * LANE, (h + 1) * LANE)
                right = slice(breadth + h * LANE, breadth + (h + 1) * LANE)
                stacked[k, top, left] = re
                stacked[k, top, right] = im
                stacked[k, low, left] = -im
                stacked[k, low, right] = re
            return carry

        lax.fori_loop(0, SIDE, interpolate, 0)


def main_kernel(
    plan_ref,
    mask_in,
    trig_in,
    stacked_in,
    steer_in,
    scene_ref,
    grad_ref,
    mask,
    omask,
    trig,
    stacked,
    steer,
    tiles,
    crecv,
    s1,
    r1a, r1b, r1c,
    s2a, s2b, s2c,
    r2a, r2b, r2c,
    s3a, s3b, s3c,
    r3a, r3b, r3c,
    units,
    wf,
    acc,
    lsem,
    msem,
    csend, crcv,
    s1send, s1recv,
    s2send, s2recv,
    s3send, s3recv,
    gsend, grecv,
    fsend, frecv,
):
    r1, s2, r2, s3, r3 = (r1a, r1b, r1c), (s2a, s2b, s2c), (r2a, r2b, r2c), (s3a, s3b, s3c), (r3a, r3b, r3c)
    where, core = position()
    y_own, z_own, x_own = turned(where, core)
    other = (y_own * 2 + 1 - core, z_own * SIDE + x_own)
    pulses = trig.shape[1]
    slots = steer.shape[0]

    for j in range(slots):
        pltpu.make_async_copy(steer_in.at[j], steer.at[j], lsem.at[j]).start()
    local = []
    for n, (src, dst) in enumerate(((mask_in, mask), (trig_in, trig), (stacked_in, stacked))):
        cp = pltpu.make_async_copy(src, dst, lsem.at[slots + n])
        cp.start()
        local.append(cp)

    barrier = pltpu.get_barrier_semaphore()
    pl.semaphore_signal(barrier, inc=1, device_id=other, device_id_type=MESH)
    for axis in range(3):
        for d in range(1, SIDE):
            pl.semaphore_signal(
                barrier, inc=1, device_id=device_at(shifted(where, axis, d), core), device_id_type=MESH
            )
    local[0].wait()
    local[1].wait()

    def turn(j, carry):
        pltpu.make_async_copy(steer_in.at[j], steer.at[j], lsem.at[j]).wait()
        cosine = trig[0:1, :]
        sines = trig[1:2, :]

        def rows(i, c2):
            at = pl.ds(pl.multiple_of(i * 64, 64), 64)
            re = steer[j, at, :pulses].astype(jnp.float32)
            im = steer[j, at, pulses:].astype(jnp.float32)
            steer[j, at, :pulses] = (re * cosine - im * sines).astype(jnp.bfloat16)
            steer[j, at, pulses:] = (re * sines + im * cosine).astype(jnp.bfloat16)
            return c2

        return lax.fori_loop(0, steer.shape[1] // 64, rows, carry)

    lax.fori_loop(0, slots, turn, 0)

    pl.semaphore_wait(barrier, 10)
    mcopy = pltpu.make_async_remote_copy(
        src_ref=mask, dst_ref=omask, send_sem=msem.at[0], recv_sem=msem.at[1], device_id=other, device_id_type=MESH
    )
    mcopy.start()
    local[2].wait()

    def core_copy(t):
        return pltpu.make_async_remote_copy(
            src_ref=tiles.at[t, :, 1 - core],
            dst_ref=crecv.at[t],
            send_sem=csend.at[t],
            recv_sem=crcv.at[t],
            device_id=other,
            device_id_type=MESH,
        )

    stage1, stage2, stage3 = {}, {}, {}

    def send1(p, d, src_fixed, key):
        lo, hi, order = PARTS[p]
        axis = order[0]
        fixed = dict(src_fixed)
        target = shifted(where, axis, d)
        fixed[axis] = target[axis]
        dst = tuple(src_fixed.get(a, slice(None)) for a in range(3) if a != axis)
        n = len(stage1)
        cp = pltpu.make_async_remote_copy(
            src_ref=s1.at[pick(fixed, lo, hi)],
            dst_ref=r1[p].at[(d - 1,) + dst],
            send_sem=s1send.at[n],
            recv_sem=s1recv.at[n],
            device_id=device_at(target, core),
            device_id_type=MESH,
        )
        cp.start()
        stage1[key] = cp

    def rest_index(p, fixed):
        return tuple(fixed.get(a, slice(None)) for a in range(3) if a != PARTS[p][2][0])

    def add_row(p, row):
        lo, hi, (a, b, c) = PARTS[p]

        def add(o, carry):
            here = rest_index(p, {b: row, c: o})
            v = s1[pick({a: where[a], b: row, c: o}, lo, hi)].astype(jnp.float32)
            for d in range(SIDE - 1):
                v = v + r1[p][(d,) + here].astype(jnp.float32)
            s2[p][here] = v.astype(jnp.bfloat16)
            return carry

        lax.fori_loop(0, SIDE, add, 0)

    def send2(p, d):
        b = PARTS[p][2][1]
        target = shifted(where, b, d)
        cp = pltpu.make_async_remote_copy(
            src_ref=s2[p].at[rest_index(p, {b: target[b]})],
            dst_ref=r2[p].at[d - 1],
            send_sem=s2send.at[p * 3 + d - 1],
            recv_sem=s2recv.at[p * 3 + d - 1],
            device_id=device_at(target, core),
            device_id_type=MESH,
        )
        cp.start()
        stage2[p, d] = cp

    def row_done(p, g):
        for d in NEAR_FIRST:
            stage1[p, g, d].wait_recv()
        add_row(p, lax.rem(where[1] + 1 + g, SIDE))
        if g < SIDE - 1:
            send2(p, g + 1)

    def send3(p):
        lo, hi, (a, b, c) = PARTS[p]
        for d in NEAR_FIRST:
            stage2[p, d].wait_recv()
        for q in range(SIDE):
            v = s2[p][rest_index(p, {b: where[b], c: q})].astype(jnp.float32)
            for d in range(SIDE - 1):
                v = v + r2[p][d, q].astype(jnp.float32)
            s3[p][q] = v
        for d in NEAR_FIRST:
            target = shifted(where, c, d)
            cp = pltpu.make_async_remote_copy(
                src_ref=s3[p].at[target[c]],
                dst_ref=r3[p].at[d - 1],
                send_sem=s3send.at[p * 3 + d - 1],
                recv_sem=s3recv.at[p * 3 + d - 1],
                device_id=device_at(target, core),
                device_id_type=MESH,
            )
            cp.start()
            stage3[p, d] = cp

    for g in range(SIDE):
        z = lax.rem(where[1] + 1 + g, SIDE)

        def compute(x, carry):
            t = z * SIDE + x
            left = steer[plan_ref[0, t]]
            right = stacked[plan_ref[1, t]]
            part = jnp.dot(left, right, preferred_element_type=jnp.float32)
            tiles[t] = part.reshape(tiles.shape[1:])
            core_copy(t).start()
            return carry

        lax.fori_loop(0, SIDE, compute, 0)
        if g == 0:
            mcopy.wait()

        def combine(x, carry):
            t = z * SIDE + x
            core_copy(t).wait_recv()
            for k in range(2):
                m = mask[pl.ds(t * 2 + k, 1), :]
                om = omask[pl.ds(t * 2 + k, 1), :]
                for lg in range(4):
                    lanes = slice(lg * LANE, (lg + 1) * LANE)
                    for y in range(SIDE):
                        v = tiles[t, y, core, :, lanes] * m + crecv[t, y, :, lanes] * om
                        u = k * 8 + lg * 2
                        s1[turned((y, z, x), core) + (slice(u, u + 2),)] = v.astype(jnp.bfloat16).reshape(2, SUB, LANE)
            return carry

        lax.fori_loop(0, SIDE, combine, 0)
        for d in NEAR_FIRST:
            send1(0, d, {1: z}, (0, g, d))
            send1(2, d, {1: z}, (2, g, d))
        if g < SIDE - 1:
            send1(1, g + 1, {}, (1, g + 1))

    def all_core(t, carry):
        core_copy(t).wait_send()
        return carry

    for g in range(2):
        row_done(0, g)
        row_done(2, g)
    for d in NEAR_FIRST:
        stage1[1, d].wait_recv()
    for d in NEAR_FIRST:
        add_row(1, lax.rem(where[2] + d, SIDE))
        send2(1, d)
    add_row(1, where[2])
    row_done(0, 2)
    row_done(2, 2)
    send3(1)
    row_done(0, 3)
    send3(0)
    row_done(2, 3)
    send3(2)
    for p in (1, 0, 2):
        lo, hi, order = PARTS[p]
        v = s3[p][where[order[2]]]
        for d in range(1, SIDE):
            stage3[p, d].wait_recv()
            v = v + r3[p][d - 1]
        units[lo:hi] = v

    for k in range(2):
        for lg in range(2):
            for rh in range(2):
                ur = k * 8 + lg * 2 + rh
                re = units[ur]
                im = units[ur + 4]
                power = re * re + im * im
                wf[(core,) + where + (ur,)] = (re * power).astype(jnp.bfloat16)
                wf[(core,) + where + (ur + 4,)] = (im * power).astype(jnp.bfloat16)
                rows = slice(rh * SUB, (rh + 1) * SUB)
                scene_ref[k, rows, lg * LANE : (lg + 1) * LANE] = re
                scene_ref[k, rows, (lg + 2) * LANE : (lg + 3) * LANE] = im

    gathers, forwards = {}, []

    def gather(p, fixed, axis, d, key):
        lo, hi, _ = PARTS[p]
        src = wf.at[(core,) + pick(fixed, lo, hi)]
        n = len(gathers)
        cp = pltpu.make_async_remote_copy(
            src_ref=src,
            dst_ref=src,
            send_sem=gsend.at[n],
            recv_sem=grecv.at[n],
            device_id=device_at(shifted(where, axis, d), core),
            device_id_type=MESH,
        )
        cp.start()
        gathers[key] = cp

    def forward(p, fixed):
        lo, hi, _ = PARTS[p]
        src = wf.at[(core,) + pick(fixed, lo, hi)]
        n = len(forwards)
        cp = pltpu.make_async_remote_copy(
            src_ref=src,
            dst_ref=src,
            send_sem=fsend.at[n],
            recv_sem=frecv.at[n],
            device_id=other,
            device_id_type=MESH,
        )
        cp.start()
        forwards.append(cp)

    def back(axis, d):
        return lax.rem(where[axis] + SIDE - d, SIDE)

    order_of = (0, 2, 1)
    for p in order_of:
        for d in NEAR_FIRST:
            gather(p, dict(enumerate(where)), PARTS[p][2][2], d, (p, "c", d))

    def row_out(p, r):
        a, b, c = PARTS[p][2]
        row = {a: where[a], b: back(b, r)}
        for d in (1, 3):
            gather(p, row, a, d, (p, r, d))
        forward(p, row)

    for p in order_of:
        a, b, c = PARTS[p][2]
        for d in NEAR_FIRST:
            gathers[p, "c", d].wait_recv()
        for d in NEAR_FIRST:
            gather(p, {a: where[a], b: where[b]}, b, d, (p, "b", d))
        row_out(p, 0)
    for d in NEAR_FIRST:
        for p in order_of:
            gathers[p, "b", d].wait_recv()
            row_out(p, d)
    rows_in = (0,) + NEAR_FIRST
    for r in rows_in:
        for p in order_of:
            a, b, c = PARTS[p][2]
            for d, half in ((1, slice(0, 2)), (3, slice(2, 4))):
                gathers[p, r, d].wait_recv()
                gather(p, {a: back(a, d), b: back(b, r), c: half}, a, d, (p, r, "far", d))
                forward(p, {a: back(a, d), b: back(b, r)})
    for r in rows_in:
        for p in order_of:
            a, b, c = PARTS[p][2]
            for d, half in ((1, slice(0, 2)), (3, slice(2, 4))):
                gathers[p, r, "far", d].wait_recv()
                forward(p, {a: back(a, 2), b: back(b, r), c: half})
    for cp in forwards:
        cp.wait_recv()

    acc[...] = jnp.zeros_like(acc)

    def backward(j, carry):
        zj = plan_ref[2, j]
        xj = plan_ref[3, j]
        kj = plan_ref[4, j]
        live = jnp.where(plan_ref[5, j] > 0, jnp.float32(1.0), jnp.float32(0.0))
        groups = []
        for lg in range(4):
            pieces = [
                wf[((c,) + ((y, zj, xj) if c == 0 else (xj, zj, y))) + (pl.ds(kj * 8 + lg * 2, 2),)].reshape(2 * SUB, LANE)
                for y in range(SIDE)
                for c in range(2)
            ]
            groups.append(jnp.concatenate(pieces, axis=0))
        weight = jnp.concatenate(groups, axis=1)
        moments = lax.dot_general(
            weight, stacked[kj], (((1,), (1,)), ((), ())), preferred_element_type=jnp.float32
        )
        re = steer[j, :, :pulses].astype(jnp.float32)
        im = steer[j, :, pulses:].astype(jnp.float32)
        term = im * moments[:, :pulses] - re * moments[:, pulses:]
        acc[...] += jnp.sum(term.reshape(-1, 8, pulses), axis=0) * live
        return carry

    lax.fori_loop(0, slots, backward, 0)
    factor = -4.0 / math.sqrt(steer.shape[1] * (stacked.shape[2] // 2))
    grad_ref[...] = jnp.sum(acc[...], axis=0, keepdims=True) * factor

    lax.fori_loop(0, 4 * SIDE, all_core, 0)
    for cp in [*stage1.values(), *stage2.values(), *stage3.values(), *gathers.values(), *forwards]:
        cp.wait_send()


def on_device(echoes, phases, kernel, steering, footprint, counts, range_start):
    columns = lax.axis_size("tile")
    row_parts = lax.axis_size("pulse")
    pulses = echoes.shape[0]
    breadth = kernel.shape[2]
    height = steering.shape[2]
    slots = steering.shape[1]
    tile_rows = range_start.shape[1]
    part_rows = height // row_parts
    width = 2 * breadth

    f32, bf16 = jnp.float32, jnp.bfloat16
    sizes = [hi - lo for lo, hi, _ in PARTS]
    vmem = pltpu.VMEM
    sem = lambda n: pltpu.SemaphoreType.DMA((n,))
    anywhere = pl.BlockSpec(memory_space=pl.ANY)
    smem = pl.BlockSpec(memory_space=pltpu.SMEM)
    whole = pl.BlockSpec(memory_space=pltpu.VMEM)
    span = kernel.shape[1] + LANE
    plan, mask, trig, stacked = pl.pallas_call(
        local_kernel,
        out_shape=(
            jax.ShapeDtypeStruct((6, columns), jnp.int32),
            jax.ShapeDtypeStruct((columns * tile_rows, LANE), f32),
            jax.ShapeDtypeStruct((2, pulses), f32),
            jax.ShapeDtypeStruct((tile_rows, 2 * pulses, width), bf16),
        ),
        in_specs=[smem] * 3 + [whole] * 2 + [anywhere],
        out_specs=[smem] + [whole] * 3,
        scratch_shapes=[
            vmem((tile_rows, pulses, 2, span), bf16),
            vmem((breadth // LANE, 2 * pulses // SIDE, LANE), f32),
            sem(2),
        ],
    )(footprint, counts, range_start, phases[None], kernel[0], echoes)
    scene, grad = pl.pallas_call(
        main_kernel,
        out_shape=(
            jax.ShapeDtypeStruct((tile_rows, part_rows, width), f32),
            jax.ShapeDtypeStruct((1, pulses), f32),
        ),
        in_specs=[smem] + [anywhere] * 4,
        out_specs=[whole] * 2,
        scratch_shapes=[
            vmem((columns * tile_rows, LANE), f32),
            vmem((columns * tile_rows, LANE), f32),
            vmem((2, pulses), f32),
            vmem((tile_rows, 2 * pulses, width), bf16),
            vmem((slots, height, 2 * pulses), bf16),
            vmem((columns, SIDE, 2, part_rows, width), f32),
            vmem((columns, SIDE, part_rows, width), f32),
            vmem((SIDE, SIDE, SIDE, 16, SUB, LANE), bf16),
        ]
        + [vmem((3, SIDE, SIDE, n, SUB, LANE), bf16) for n in sizes]
        + [vmem((SIDE, SIDE, n, SUB, LANE), bf16) for n in sizes]
        + [vmem((3, SIDE, n, SUB, LANE), bf16) for n in sizes]
        + [vmem((SIDE, n, SUB, LANE), f32) for n in sizes]
        + [vmem((3, n, SUB, LANE), f32) for n in sizes]
        + [
            vmem((16, SUB, LANE), f32),
            vmem((2, SIDE, SIDE, SIDE, 16, SUB, LANE), bf16),
            vmem((8, pulses), f32),
            sem(slots + 3),
            sem(2),
            sem(columns), sem(columns),
            sem(27), sem(27),
            sem(9), sem(9),
            sem(9), sem(9),
            sem(66), sem(66),
            sem(60), sem(60),
        ],
        compiler_params=pltpu.CompilerParams(
            collective_id=0, has_side_effects=True, vmem_limit_bytes=60 << 20
        ),
    )(plan, mask, trig, stacked, steering[0])
    return (scene[:, None], grad[0])


def solution(mesh):
    placed = (
        P(("pulse", "tile"), None, None),
        P(("pulse", "tile")),
        P(("pulse", "tile"), None, None),
        P(("pulse", "tile"), None, None, None),
        P(("pulse", "tile"), None),
        P(("pulse", "tile")),
        P(("pulse", "tile"), None),
    )
    return jax.shard_map(
        on_device,
        mesh=mesh,
        in_specs=placed,
        out_specs=(P(None, "tile", "pulse", None), P(("pulse", "tile"))),
        check_vma=False,
    )
```

```python
import functools
import math

import jax
import jax.numpy as jnp
from jax import lax
from jax.experimental import pallas as pl
from jax.experimental.pallas import tpu as pltpu
from jax.sharding import PartitionSpec as P

MESH = pl.DeviceIdType.MESH
SIDE = 4
LANE = 128
SUB = 16
PARTS = (
    (0, 6, (0, 1, 2)),
    (6, 10, (1, 2, 0)),
    (10, 16, (2, 1, 0)),
)
GATHER_PARTS = (
    (0, 5, (0, 1, 2)),
    (5, 10, (1, 2, 0)),
    (10, 16, (2, 0, 1)),
)
NEAR_FIRST = (1, 3, 2)
LAST_ROW = 2
LAG = 2


def position():
    p = lax.axis_index("pulse")
    t = lax.axis_index("tile")
    core = p % 2
    return turned((p // 2, t // SIDE, t % SIDE), core), core


def turned(place, core):
    first = jnp.where(core == 0, place[0], place[2])
    last = jnp.where(core == 0, place[2], place[0])
    return (first, place[1], last)


def device_at(where, core):
    y, z, x = turned(where, core)
    return (y * 2 + core, z * SIDE + x)


def shifted(where, axis, d):
    moved = list(where)
    moved[axis] = lax.rem(where[axis] + d, SIDE)
    return tuple(moved)


def pick(fixed, lo, hi):
    return tuple(fixed.get(a, slice(None)) for a in range(3)) + (slice(lo, hi),)


def local_kernel(
    foot_ref,
    count_ref,
    start_ref,
    phases_ref,
    kernel_ref,
    echoes_in,
    plan_ref,
    mask,
    trig,
    stacked,
    windows,
    raw,
    sem,
):
    pulses = phases_ref.shape[1]
    window_len, breadth = kernel_ref.shape
    span = window_len + LANE
    last = (echoes_in.shape[2] - span) // LANE
    slots = foot_ref.shape[1]
    blocks = [jnp.minimum(start_ref[0, k] // LANE, last) for k in range(2)]
    copies = []
    for k in range(2):
        cp = pltpu.make_async_copy(
            echoes_in.at[:, :, pl.ds(pl.multiple_of(blocks[k] * LANE, LANE), span)], windows.at[k], sem.at[k]
        )
        cp.start()
        copies.append(cp)
    count = count_ref[0]
    for t in range(SIDE * SIDE):
        for n in range(6):
            plan_ref[n, t] = jnp.int32(0)
    tile_id = lax.broadcasted_iota(jnp.int32, mask.shape, 0)
    tile_id = tile_id // 2 + tile_id % 2 * (SIDE * SIDE)
    found = jnp.zeros(mask.shape, jnp.float32)
    for j in range(slots):
        name = foot_ref[0, j]
        live = j < count
        found = jnp.where(tile_id == jnp.where(live, name, -1), jnp.float32(1.0), found)
        plan_ref[2, j] = name // SIDE % SIDE
        plan_ref[3, j] = name % SIDE
        plan_ref[4, j] = name // (SIDE * SIDE)
        plan_ref[5, j] = live.astype(jnp.int32)

        @pl.when(live)
        def _():
            t = name % (SIDE * SIDE)
            plan_ref[0, t] = jnp.int32(j)
            plan_ref[1, t] = name // (SIDE * SIDE)

    mask[...] = found
    angle = phases_ref[...]
    trig[0:1, :] = jnp.cos(angle)
    trig[1:2, :] = jnp.sin(angle)
    depth = pulses // SIDE
    for k in range(2):
        weights = jnp.concatenate(
            [kernel_ref[...].astype(jnp.float32), jnp.zeros((LANE, breadth), jnp.float32)], axis=0
        )
        weights = pltpu.roll(weights, start_ref[0, k] - blocks[k] * LANE, 0).astype(jnp.bfloat16)
        copies[k].wait()

        def interpolate(i, carry):
            at = pl.multiple_of(i * depth, depth)
            window = windows[k, pl.ds(at, depth)]
            value = jnp.dot(window.reshape(2 * depth, span), weights, preferred_element_type=jnp.float32)
            top, low = pl.ds(at, depth), pl.ds(pulses + at, depth)
            for h in range(breadth // LANE):
                raw[h] = value[:, h * LANE : (h + 1) * LANE]
                re = raw[h, pl.ds(0, depth, stride=2), :].astype(jnp.bfloat16)
                im = raw[h, pl.ds(1, depth, stride=2), :].astype(jnp.bfloat16)
                left = slice(h * LANE, (h + 1) * LANE)
                right = slice(breadth + h * LANE, breadth + (h + 1) * LANE)
                stacked[k, top, left] = re
                stacked[k, top, right] = im
                stacked[k, low, left] = -im
                stacked[k, low, right] = re
            return carry

        lax.fori_loop(0, SIDE, interpolate, 0)


def main_kernel(
    plan_ref,
    mask_in,
    trig_in,
    stacked_in,
    steer_in,
    scene_ref,
    grad_ref,
    mask,
    omask,
    trig,
    stacked,
    steer,
    tiles,
    crecv,
    s1,
    r1a, r1b, r1c,
    s2a, s2b, s2c,
    r2a, r2b, r2c,
    s3a, s3b, s3c,
    r3a, r3b, r3c,
    units,
    wf,
    acc,
    lsem,
    msem,
    csend, crcv,
    s1send, s1recv,
    s2send, s2recv,
    s3send, s3recv,
    gsend, grecv,
    fsend, frecv,
):
    r1, s2, r2, s3, r3 = (r1a, r1b, r1c), (s2a, s2b, s2c), (r2a, r2b, r2c), (s3a, s3b, s3c), (r3a, r3b, r3c)
    where, core = position()
    y_own, z_own, x_own = turned(where, core)
    other = (y_own * 2 + 1 - core, z_own * SIDE + x_own)
    pulses = trig.shape[1]
    slots = steer.shape[0]

    for j in range(slots):
        pltpu.make_async_copy(steer_in.at[j], steer.at[j], lsem.at[j]).start()
    local = []
    for n, (src, dst) in enumerate(((mask_in, mask), (trig_in, trig), (stacked_in, stacked))):
        cp = pltpu.make_async_copy(src, dst, lsem.at[slots + n])
        cp.start()
        local.append(cp)

    barrier = pltpu.get_barrier_semaphore()
    pl.semaphore_signal(barrier, inc=1, device_id=other, device_id_type=MESH)
    for axis in range(3):
        for d in range(1, SIDE):
            pl.semaphore_signal(
                barrier, inc=1, device_id=device_at(shifted(where, axis, d), core), device_id_type=MESH
            )
    local[0].wait()
    local[1].wait()

    def turn(j, carry):
        pltpu.make_async_copy(steer_in.at[j], steer.at[j], lsem.at[j]).wait()
        cosine = trig[0:1, :]
        sines = trig[1:2, :]

        def rows(i, c2):
            at = pl.ds(pl.multiple_of(i * 64, 64), 64)
            re = steer[j, at, :pulses].astype(jnp.float32)
            im = steer[j, at, pulses:].astype(jnp.float32)
            steer[j, at, :pulses] = (re * cosine - im * sines).astype(jnp.bfloat16)
            steer[j, at, pulses:] = (re * sines + im * cosine).astype(jnp.bfloat16)
            return c2

        return lax.fori_loop(0, steer.shape[1] // 64, rows, carry)

    lax.fori_loop(0, slots, turn, 0)

    pl.semaphore_wait(barrier, 10)
    mcopy = pltpu.make_async_remote_copy(
        src_ref=mask, dst_ref=omask, send_sem=msem.at[0], recv_sem=msem.at[1], device_id=other, device_id_type=MESH
    )
    mcopy.start()
    local[2].wait()

    def core_copy(t):
        return pltpu.make_async_remote_copy(
            src_ref=tiles.at[t, :, 1 - core],
            dst_ref=crecv.at[t],
            send_sem=csend.at[0],
            recv_sem=crcv.at[t],
            device_id=other,
            device_id_type=MESH,
        )

    stage1, stage2, stage3 = {}, {}, {}

    def send1(p, d, src_fixed, key):
        lo, hi, order = PARTS[p]
        axis = order[0]
        fixed = dict(src_fixed)
        target = shifted(where, axis, d)
        fixed[axis] = target[axis]
        dst = tuple(src_fixed.get(a, slice(None)) for a in range(3) if a != axis)
        n = len(stage1)
        cp = pltpu.make_async_remote_copy(
            src_ref=s1.at[pick(fixed, lo, hi)],
            dst_ref=r1[p].at[(d - 1,) + dst],
            send_sem=s1send.at[0],
            recv_sem=s1recv.at[n],
            device_id=device_at(target, core),
            device_id_type=MESH,
        )
        cp.start()
        stage1[key] = cp

    def rest_index(p, fixed):
        return tuple(fixed.get(a, slice(None)) for a in range(3) if a != PARTS[p][2][0])

    def add_row(p, row):
        lo, hi, (a, b, c) = PARTS[p]

        def add(o, carry):
            here = rest_index(p, {b: row, c: o})
            v = s1[pick({a: where[a], b: row, c: o}, lo, hi)].astype(jnp.float32)
            for d in range(SIDE - 1):
                v = v + r1[p][(d,) + here].astype(jnp.float32)
            s2[p][here] = v.astype(jnp.bfloat16)
            return carry

        lax.fori_loop(0, SIDE, add, 0)

    def send2(p, d):
        b = PARTS[p][2][1]
        target = shifted(where, b, d)
        cp = pltpu.make_async_remote_copy(
            src_ref=s2[p].at[rest_index(p, {b: target[b]})],
            dst_ref=r2[p].at[d - 1],
            send_sem=s2send.at[0],
            recv_sem=s2recv.at[p * 3 + d - 1],
            device_id=device_at(target, core),
            device_id_type=MESH,
        )
        cp.start()
        stage2[p, d] = cp

    def row_done(p, g):
        for d in NEAR_FIRST:
            stage1[p, g, d].wait_recv()
        add_row(p, lax.rem(where[1] + 1 + g, SIDE))
        if g < SIDE - 1:
            send2(p, g + 1)

    def send3(p):
        lo, hi, (a, b, c) = PARTS[p]
        for d in NEAR_FIRST:
            stage2[p, d].wait_recv()
        for q in range(SIDE):
            v = s2[p][rest_index(p, {b: where[b], c: q})].astype(jnp.float32)
            for d in range(SIDE - 1):
                v = v + r2[p][d, q].astype(jnp.float32)
            s3[p][q] = v
        for d in NEAR_FIRST:
            target = shifted(where, c, d)
            cp = pltpu.make_async_remote_copy(
                src_ref=s3[p].at[target[c]],
                dst_ref=r3[p].at[d - 1],
                send_sem=s3send.at[p],
                recv_sem=s3recv.at[p * 3 + d - 1],
                device_id=device_at(target, core),
                device_id_type=MESH,
            )
            cp.start()
            stage3[p, d] = cp

    def column(i):
        return lax.rem(where[1] + 1 + i // SIDE, SIDE), i % SIDE

    def compute(i):
        z, x = column(i)
        t = z * SIDE + x
        left = steer[plan_ref[0, t]]
        right = stacked[plan_ref[1, t]]
        part = jnp.dot(left, right, preferred_element_type=jnp.float32)
        tiles[t] = part.reshape(tiles.shape[1:])
        core_copy(t).start()

    def combine(i):
        z, x = column(i)
        t = z * SIDE + x
        core_copy(t).wait_recv()
        for k in range(2):
            m = mask[pl.ds(t * 2 + k, 1), :]
            om = omask[pl.ds(t * 2 + k, 1), :]
            for lg in range(4):
                lanes = slice(lg * LANE, (lg + 1) * LANE)
                for y in range(SIDE):
                    v = tiles[t, y, core, :, lanes] * m + crecv[t, y, :, lanes] * om
                    u = k * 8 + lg * 2
                    s1[turned((y, z, x), core) + (slice(u, u + 2),)] = v.astype(jnp.bfloat16).reshape(2, SUB, LANE)

    def send_group(g):
        z = lax.rem(where[1] + 1 + g, SIDE)
        for d in NEAR_FIRST:
            send1(0, d, {1: z}, (0, g, d))
            send1(2, d, {1: z}, (2, g, d))
        if g < SIDE - 1:
            send1(1, g + 1, {}, (1, g + 1))

    def both(i, carry):
        compute(i)
        combine(i - LAG)
        return carry

    def first(i, carry):
        compute(i)
        return carry

    def final(i, carry):
        combine(i)
        return carry

    total = SIDE * SIDE
    lax.fori_loop(0, LAG, first, 0)
    mcopy.wait()
    lax.fori_loop(LAG, SIDE + LAG, both, 0)
    send_group(0)
    lax.fori_loop(SIDE + LAG, 2 * SIDE + LAG, both, 0)
    send_group(1)
    lax.fori_loop(2 * SIDE + LAG, 3 * SIDE + LAG, both, 0)
    send_group(2)
    lax.fori_loop(3 * SIDE + LAG, total, both, 0)
    lax.fori_loop(total - LAG, total, final, 0)
    send_group(3)

    for g in range(2):
        row_done(0, g)
        row_done(2, g)
    for d in NEAR_FIRST:
        stage1[1, d].wait_recv()
    for d in NEAR_FIRST:
        add_row(1, lax.rem(where[2] + d, SIDE))
        send2(1, d)
    add_row(1, where[2])
    row_done(0, 2)
    row_done(2, 2)
    send3(1)
    row_done(0, 3)
    send3(0)
    row_done(2, 3)
    send3(2)
    for p in (1, 0, 2):
        lo, hi, order = PARTS[p]
        v = s3[p][where[order[2]]]
        for d in range(1, SIDE):
            stage3[p, d].wait_recv()
            v = v + r3[p][d - 1]
        units[lo:hi] = v

    for k in range(2):
        for lg in range(2):
            for rh in range(2):
                ur = k * 8 + lg * 2 + rh
                re = units[ur]
                im = units[ur + 4]
                power = re * re + im * im
                wf[(core,) + where + (ur,)] = (re * power).astype(jnp.bfloat16)
                wf[(core,) + where + (ur + 4,)] = (im * power).astype(jnp.bfloat16)
                rows = slice(rh * SUB, (rh + 1) * SUB)
                scene_ref[k, rows, lg * LANE : (lg + 1) * LANE] = re
                scene_ref[k, rows, (lg + 2) * LANE : (lg + 3) * LANE] = im

    gathers = {}

    def gather(p, fixed, axis, d, key, step):
        lo, hi, _ = GATHER_PARTS[p]
        src = wf.at[(core,) + pick(fixed, lo, hi)]
        n = len(gathers)
        cp = pltpu.make_async_remote_copy(
            src_ref=src,
            dst_ref=src,
            send_sem=gsend.at[step],
            recv_sem=grecv.at[n],
            device_id=device_at(shifted(where, axis, d), core),
            device_id_type=MESH,
        )
        cp.start()
        gathers[key] = cp

    def forward(p, fixed):
        lo, hi, _ = GATHER_PARTS[p]
        src = wf.at[(core,) + pick(fixed, lo, hi)]
        cp = pltpu.make_async_remote_copy(
            src_ref=src,
            dst_ref=src,
            send_sem=fsend.at[0],
            recv_sem=frecv.at[0],
            device_id=other,
            device_id_type=MESH,
        )
        cp.start()

    def back(axis, d):
        return lax.rem(where[axis] + SIDE - d, SIDE)

    order_of = (2, 0, 1)
    for p in order_of:
        for d in NEAR_FIRST:
            gather(p, dict(enumerate(where)), GATHER_PARTS[p][2][2], d, (p, "c", d), 0)

    def row_out(p, r):
        a, b, c = GATHER_PARTS[p][2]
        row = {a: where[a], b: back(b, r)}
        for d in NEAR_FIRST if r == LAST_ROW else (1, 3):
            gather(p, row, a, d, (p, r, d), 2)
        forward(p, row)

    for p in order_of:
        a, b, c = GATHER_PARTS[p][2]
        for d in NEAR_FIRST:
            gathers[p, "c", d].wait_recv()
        for d in NEAR_FIRST:
            gather(p, {a: where[a], b: where[b]}, b, d, (p, "b", d), 1)
        row_out(p, 0)
    for d in NEAR_FIRST:
        for p in order_of:
            gathers[p, "b", d].wait_recv()
            row_out(p, d)
    for r in (0, 1, 3):
        for p in order_of:
            a, b, c = GATHER_PARTS[p][2]
            for d, half in ((1, slice(0, 2)), (3, slice(2, 4))):
                gathers[p, r, d].wait_recv()
                gather(p, {a: back(a, d), b: back(b, r), c: half}, a, d, (p, r, "far", d), 2)
                forward(p, {a: back(a, d), b: back(b, r)})
    for r in (0, 1, 3):
        for p in order_of:
            a, b, c = GATHER_PARTS[p][2]
            for d in (1, 3):
                gathers[p, r, "far", d].wait_recv()
            forward(p, {a: back(a, 2), b: back(b, r)})
    for d in NEAR_FIRST:
        for p in order_of:
            a, b, c = GATHER_PARTS[p][2]
            gathers[p, LAST_ROW, d].wait_recv()
            forward(p, {a: back(a, d), b: back(b, LAST_ROW)})
    pltpu.make_async_copy(wf.at[1 - core], wf.at[1 - core], frecv.at[0]).wait()

    acc[...] = jnp.zeros_like(acc)

    def backward(j, carry):
        zj = plan_ref[2, j]
        xj = plan_ref[3, j]
        kj = plan_ref[4, j]
        live = jnp.where(plan_ref[5, j] > 0, jnp.float32(1.0), jnp.float32(0.0))
        groups = []
        for lg in range(4):
            pieces = [
                wf[((c,) + ((y, zj, xj) if c == 0 else (xj, zj, y))) + (pl.ds(kj * 8 + lg * 2, 2),)].reshape(2 * SUB, LANE)
                for y in range(SIDE)
                for c in range(2)
            ]
            groups.append(jnp.concatenate(pieces, axis=0))
        weight = jnp.concatenate(groups, axis=1)
        moments = lax.dot_general(
            weight, stacked[kj], (((1,), (1,)), ((), ())), preferred_element_type=jnp.float32
        )
        re = steer[j, :, :pulses].astype(jnp.float32)
        im = steer[j, :, pulses:].astype(jnp.float32)
        term = im * moments[:, :pulses] - re * moments[:, pulses:]
        acc[...] += jnp.sum(term.reshape(-1, 8, pulses), axis=0) * live
        return carry

    lax.fori_loop(0, slots, backward, 0, unroll=4)
    factor = -4.0 / math.sqrt(steer.shape[1] * (stacked.shape[2] // 2))
    grad_ref[...] = jnp.sum(acc[...], axis=0, keepdims=True) * factor

    def all_sent(like, sem):
        pltpu.make_async_copy(like, like, sem).wait()

    all_sent(crecv, csend.at[0])
    all_sent(s1.at[:3], s1send.at[0])
    all_sent(s1.at[0, :3], s2send.at[0])
    for p in range(3):
        all_sent(r3[p], s3send.at[p])
    all_sent(wf.at[0, 0, 0, :3], gsend.at[0])
    all_sent(wf.at[0, 0, :3], gsend.at[1])
    all_sent(wf.at[0, :3], gsend.at[2])
    all_sent(wf.at[core], fsend.at[0])


def on_device(echoes, phases, kernel, steering, footprint, counts, range_start):
    columns = lax.axis_size("tile")
    row_parts = lax.axis_size("pulse")
    pulses = echoes.shape[0]
    breadth = kernel.shape[2]
    height = steering.shape[2]
    slots = steering.shape[1]
    tile_rows = range_start.shape[1]
    part_rows = height // row_parts
    width = 2 * breadth

    f32, bf16 = jnp.float32, jnp.bfloat16
    sizes = [hi - lo for lo, hi, _ in PARTS]
    vmem = pltpu.VMEM
    sem = lambda n: pltpu.SemaphoreType.DMA((n,))
    anywhere = pl.BlockSpec(memory_space=pl.ANY)
    smem = pl.BlockSpec(memory_space=pltpu.SMEM)
    whole = pl.BlockSpec(memory_space=pltpu.VMEM)
    span = kernel.shape[1] + LANE
    plan, mask, trig, stacked = pl.pallas_call(
        local_kernel,
        out_shape=(
            jax.ShapeDtypeStruct((6, columns), jnp.int32),
            jax.ShapeDtypeStruct((columns * tile_rows, LANE), f32),
            jax.ShapeDtypeStruct((2, pulses), f32),
            jax.ShapeDtypeStruct((tile_rows, 2 * pulses, width), bf16),
        ),
        in_specs=[smem] * 3 + [whole] * 2 + [anywhere],
        out_specs=[smem] + [whole] * 3,
        scratch_shapes=[
            vmem((tile_rows, pulses, 2, span), bf16),
            vmem((breadth // LANE, 2 * pulses // SIDE, LANE), f32),
            sem(2),
        ],
    )(footprint, counts, range_start, phases[None], kernel[0], echoes)
    scene, grad = pl.pallas_call(
        main_kernel,
        out_shape=(
            jax.ShapeDtypeStruct((tile_rows, part_rows, width), f32),
            jax.ShapeDtypeStruct((1, pulses), f32),
        ),
        in_specs=[smem] + [anywhere] * 4,
        out_specs=[whole] * 2,
        scratch_shapes=[
            vmem((columns * tile_rows, LANE), f32),
            vmem((columns * tile_rows, LANE), f32),
            vmem((2, pulses), f32),
            vmem((tile_rows, 2 * pulses, width), bf16),
            vmem((slots, height, 2 * pulses), bf16),
            vmem((columns, SIDE, 2, part_rows, width), f32),
            vmem((columns, SIDE, part_rows, width), f32),
            vmem((SIDE, SIDE, SIDE, 16, SUB, LANE), bf16),
        ]
        + [vmem((3, SIDE, SIDE, n, SUB, LANE), bf16) for n in sizes]
        + [vmem((SIDE, SIDE, n, SUB, LANE), bf16) for n in sizes]
        + [vmem((3, SIDE, n, SUB, LANE), bf16) for n in sizes]
        + [vmem((SIDE, n, SUB, LANE), f32) for n in sizes]
        + [vmem((3, n, SUB, LANE), f32) for n in sizes]
        + [
            vmem((16, SUB, LANE), f32),
            vmem((2, SIDE, SIDE, SIDE, 16, SUB, LANE), bf16),
            vmem((8, pulses), f32),
            sem(slots + 3),
            sem(2),
            sem(1), sem(columns),
            sem(1), sem(27),
            sem(1), sem(9),
            sem(3), sem(9),
            sem(3), sem(66),
            sem(1), sem(1),
        ],
        compiler_params=pltpu.CompilerParams(
            collective_id=0, has_side_effects=True, vmem_limit_bytes=60 << 20
        ),
    )(plan, mask, trig, stacked, steering[0])
    return (scene[:, None], grad[0])


def solution(mesh):
    placed = (
        P(("pulse", "tile"), None, None),
        P(("pulse", "tile")),
        P(("pulse", "tile"), None, None),
        P(("pulse", "tile"), None, None, None),
        P(("pulse", "tile"), None),
        P(("pulse", "tile")),
        P(("pulse", "tile"), None),
    )
    return jax.shard_map(
        on_device,
        mesh=mesh,
        in_specs=placed,
        out_specs=(P(None, "tile", "pulse", None), P(("pulse", "tile"))),
        check_vma=False,
    )
```

```python
import functools
import math

import jax
import jax.numpy as jnp
from jax import lax
from jax.experimental import pallas as pl
from jax.experimental.pallas import tpu as pltpu
from jax.sharding import PartitionSpec as P

MESH = pl.DeviceIdType.MESH
SIDE = 4
LANE = 128
SUB = 16
PARTS = (
    (0, 6, (0, 1, 2)),
    (6, 10, (1, 2, 0)),
    (10, 16, (2, 1, 0)),
)
GATHER_PARTS = (
    (0, 5, (0, 1, 2)),
    (5, 10, (1, 2, 0)),
    (10, 16, (2, 0, 1)),
)
NEAR_FIRST = (1, 3, 2)
LAST_ROW = 2
LAG = 2


def position():
    p = lax.axis_index("pulse")
    t = lax.axis_index("tile")
    core = p % 2
    return turned((p // 2, t // SIDE, t % SIDE), core), core


def turned(place, core):
    first = jnp.where(core == 0, place[0], place[2])
    last = jnp.where(core == 0, place[2], place[0])
    return (first, place[1], last)


def device_at(where, core):
    y, z, x = turned(where, core)
    return (y * 2 + core, z * SIDE + x)


def shifted(where, axis, d):
    moved = list(where)
    moved[axis] = lax.rem(where[axis] + d, SIDE)
    return tuple(moved)


def pick(fixed, lo, hi):
    return tuple(fixed.get(a, slice(None)) for a in range(3)) + (slice(lo, hi),)


def local_kernel(
    foot_ref,
    count_ref,
    start_ref,
    phases_ref,
    kernel_ref,
    echoes_in,
    plan_ref,
    mask,
    trig,
    stacked_out,
    stacked,
    windows,
    raw,
    sem,
):
    pulses = phases_ref.shape[1]
    window_len, breadth = kernel_ref.shape
    span = window_len + LANE
    last = (echoes_in.shape[2] - span) // LANE
    slots = foot_ref.shape[1]
    blocks = [jnp.minimum(start_ref[0, k] // LANE, last) for k in range(2)]
    copies, outs = [], []
    for k in range(2):
        cp = pltpu.make_async_copy(
            echoes_in.at[:, :, pl.ds(pl.multiple_of(blocks[k] * LANE, LANE), span)], windows.at[k], sem.at[k]
        )
        cp.start()
        copies.append(cp)
    count = count_ref[0]
    for t in range(SIDE * SIDE):
        for n in range(6):
            plan_ref[n, t] = jnp.int32(0)
    tile_id = lax.broadcasted_iota(jnp.int32, mask.shape, 0)
    tile_id = tile_id // 2 + tile_id % 2 * (SIDE * SIDE)
    found = jnp.zeros(mask.shape, jnp.float32)
    for j in range(slots):
        name = foot_ref[0, j]
        live = j < count
        found = jnp.where(tile_id == jnp.where(live, name, -1), jnp.float32(1.0), found)
        plan_ref[2, j] = name // SIDE % SIDE
        plan_ref[3, j] = name % SIDE
        plan_ref[4, j] = name // (SIDE * SIDE)
        plan_ref[5, j] = live.astype(jnp.int32)

        @pl.when(live)
        def _():
            t = name % (SIDE * SIDE)
            plan_ref[0, t] = jnp.int32(j)
            plan_ref[1, t] = name // (SIDE * SIDE)

    mask[...] = found
    angle = phases_ref[...]
    trig[0:1, :] = jnp.cos(angle)
    trig[1:2, :] = jnp.sin(angle)
    depth = pulses // SIDE
    for k in range(2):
        weights = jnp.concatenate(
            [kernel_ref[...].astype(jnp.float32), jnp.zeros((LANE, breadth), jnp.float32)], axis=0
        )
        weights = pltpu.roll(weights, start_ref[0, k] - blocks[k] * LANE, 0).astype(jnp.bfloat16)
        copies[k].wait()

        for i in range(SIDE):
            at = i * depth
            window = windows[k, pl.ds(at, depth)]
            value = jnp.dot(window.reshape(2 * depth, span), weights, preferred_element_type=jnp.float32)
            top, low = pl.ds(at, depth), pl.ds(pulses + at, depth)
            for h in range(breadth // LANE):
                raw[i, h] = value[:, h * LANE : (h + 1) * LANE]
                re = raw[i, h, pl.ds(0, depth, stride=2), :].astype(jnp.bfloat16)
                im = raw[i, h, pl.ds(1, depth, stride=2), :].astype(jnp.bfloat16)
                left = slice(h * LANE, (h + 1) * LANE)
                right = slice(breadth + h * LANE, breadth + (h + 1) * LANE)
                stacked[k, top, left] = re
                stacked[k, top, right] = im
                stacked[k, low, left] = -im
                stacked[k, low, right] = re
        out = pltpu.make_async_copy(stacked.at[k], stacked_out.at[k], sem.at[2 + k])
        out.start()
        outs.append(out)
    for out in outs:
        out.wait()


def main_kernel(
    plan_ref,
    mask_in,
    trig_in,
    stacked_in,
    steer_in,
    scene_ref,
    grad_ref,
    mask,
    omask,
    trig,
    stacked,
    steer,
    tiles,
    crecv,
    s1,
    r1a, r1b, r1c,
    s2a, s2b, s2c,
    r2a, r2b, r2c,
    s3a, s3b, s3c,
    r3a, r3b, r3c,
    units,
    wf,
    acc,
    lsem,
    msem,
    csend, crcv,
    s1send, s1recv,
    s2send, s2recv,
    s3send, s3recv,
    gsend, grecv,
    fsend, frecv,
):
    r1, s2, r2, s3, r3 = (r1a, r1b, r1c), (s2a, s2b, s2c), (r2a, r2b, r2c), (s3a, s3b, s3c), (r3a, r3b, r3c)
    where, core = position()
    y_own, z_own, x_own = turned(where, core)
    other = (y_own * 2 + 1 - core, z_own * SIDE + x_own)
    pulses = trig.shape[1]
    slots = steer.shape[0]

    for j in range(slots):
        pltpu.make_async_copy(steer_in.at[j], steer.at[j], lsem.at[j]).start()
    local = []
    for n, (src, dst) in enumerate(((mask_in, mask), (trig_in, trig), (stacked_in, stacked))):
        cp = pltpu.make_async_copy(src, dst, lsem.at[slots + n])
        cp.start()
        local.append(cp)

    barrier = pltpu.get_barrier_semaphore()
    pl.semaphore_signal(barrier, inc=1, device_id=other, device_id_type=MESH)
    for axis in range(3):
        for d in range(1, SIDE):
            pl.semaphore_signal(
                barrier, inc=1, device_id=device_at(shifted(where, axis, d), core), device_id_type=MESH
            )
    local[0].wait()
    local[1].wait()

    def turn(j, carry):
        pltpu.make_async_copy(steer_in.at[j], steer.at[j], lsem.at[j]).wait()
        cosine = trig[0:1, :]
        sines = trig[1:2, :]

        def rows(i, c2):
            at = pl.ds(pl.multiple_of(i * 64, 64), 64)
            re = steer[j, at, :pulses].astype(jnp.float32)
            im = steer[j, at, pulses:].astype(jnp.float32)
            steer[j, at, :pulses] = (re * cosine - im * sines).astype(jnp.bfloat16)
            steer[j, at, pulses:] = (re * sines + im * cosine).astype(jnp.bfloat16)
            return c2

        return lax.fori_loop(0, steer.shape[1] // 64, rows, carry)

    lax.fori_loop(0, slots, turn, 0)

    pl.semaphore_wait(barrier, 10)
    mcopy = pltpu.make_async_remote_copy(
        src_ref=mask, dst_ref=omask, send_sem=msem.at[0], recv_sem=msem.at[1], device_id=other, device_id_type=MESH
    )
    mcopy.start()
    local[2].wait()

    def core_copy(t):
        return pltpu.make_async_remote_copy(
            src_ref=tiles.at[t, :, 1 - core],
            dst_ref=crecv.at[t],
            send_sem=csend.at[0],
            recv_sem=crcv.at[t],
            device_id=other,
            device_id_type=MESH,
        )

    stage1, stage2, stage3 = {}, {}, {}

    def send1(p, d, src_fixed, key):
        lo, hi, order = PARTS[p]
        axis = order[0]
        fixed = dict(src_fixed)
        target = shifted(where, axis, d)
        fixed[axis] = target[axis]
        dst = tuple(src_fixed.get(a, slice(None)) for a in range(3) if a != axis)
        n = len(stage1)
        cp = pltpu.make_async_remote_copy(
            src_ref=s1.at[pick(fixed, lo, hi)],
            dst_ref=r1[p].at[(d - 1,) + dst],
            send_sem=s1send.at[0],
            recv_sem=s1recv.at[n],
            device_id=device_at(target, core),
            device_id_type=MESH,
        )
        cp.start()
        stage1[key] = cp

    def rest_index(p, fixed):
        return tuple(fixed.get(a, slice(None)) for a in range(3) if a != PARTS[p][2][0])

    def add_row(p, row):
        lo, hi, (a, b, c) = PARTS[p]

        def add(o, carry):
            here = rest_index(p, {b: row, c: o})
            v = s1[pick({a: where[a], b: row, c: o}, lo, hi)].astype(jnp.float32)
            for d in range(SIDE - 1):
                v = v + r1[p][(d,) + here].astype(jnp.float32)
            s2[p][here] = v.astype(jnp.bfloat16)
            return carry

        lax.fori_loop(0, SIDE, add, 0, unroll=True)

    def send2(p, d):
        b = PARTS[p][2][1]
        target = shifted(where, b, d)
        cp = pltpu.make_async_remote_copy(
            src_ref=s2[p].at[rest_index(p, {b: target[b]})],
            dst_ref=r2[p].at[d - 1],
            send_sem=s2send.at[0],
            recv_sem=s2recv.at[p * 3 + d - 1],
            device_id=device_at(target, core),
            device_id_type=MESH,
        )
        cp.start()
        stage2[p, d] = cp

    def row_done(p, g):
        for d in NEAR_FIRST:
            stage1[p, g, d].wait_recv()
        add_row(p, lax.rem(where[1] + 1 + g, SIDE))
        if g < SIDE - 1:
            send2(p, g + 1)

    def send3(p):
        lo, hi, (a, b, c) = PARTS[p]
        for d in NEAR_FIRST:
            stage2[p, d].wait_recv()
        for q in range(SIDE):
            v = s2[p][rest_index(p, {b: where[b], c: q})].astype(jnp.float32)
            for d in range(SIDE - 1):
                v = v + r2[p][d, q].astype(jnp.float32)
            s3[p][q] = v
        for d in NEAR_FIRST:
            target = shifted(where, c, d)
            cp = pltpu.make_async_remote_copy(
                src_ref=s3[p].at[target[c]],
                dst_ref=r3[p].at[d - 1],
                send_sem=s3send.at[p],
                recv_sem=s3recv.at[p * 3 + d - 1],
                device_id=device_at(target, core),
                device_id_type=MESH,
            )
            cp.start()
            stage3[p, d] = cp

    def column(i):
        return lax.rem(where[1] + 1 + i // SIDE, SIDE), i % SIDE

    def compute(i):
        z, x = column(i)
        t = z * SIDE + x
        left = steer[plan_ref[0, t]]
        right = stacked[plan_ref[1, t]]
        part = jnp.dot(left, right, preferred_element_type=jnp.float32)
        tiles[t] = part.reshape(tiles.shape[1:])
        core_copy(t).start()

    def combine(i):
        z, x = column(i)
        t = z * SIDE + x
        core_copy(t).wait_recv()
        for k in range(2):
            m = mask[pl.ds(t * 2 + k, 1), :]
            om = omask[pl.ds(t * 2 + k, 1), :]
            for lg in range(4):
                lanes = slice(lg * LANE, (lg + 1) * LANE)
                for y in range(SIDE):
                    v = tiles[t, y, core, :, lanes] * m + crecv[t, y, :, lanes] * om
                    u = k * 8 + lg * 2
                    s1[turned((y, z, x), core) + (slice(u, u + 2),)] = v.astype(jnp.bfloat16).reshape(2, SUB, LANE)

    def send_group(g):
        z = lax.rem(where[1] + 1 + g, SIDE)
        for d in NEAR_FIRST:
            send1(0, d, {1: z}, (0, g, d))
            send1(2, d, {1: z}, (2, g, d))
        if g < SIDE - 1:
            send1(1, g + 1, {}, (1, g + 1))

    def both(i, carry):
        compute(i)
        combine(i - LAG)
        return carry

    def first(i, carry):
        compute(i)
        return carry

    def final(i, carry):
        combine(i)
        return carry

    total = SIDE * SIDE
    lax.fori_loop(0, LAG, first, 0, unroll=2)
    mcopy.wait()
    lax.fori_loop(LAG, SIDE + LAG, both, 0, unroll=2)
    send_group(0)
    lax.fori_loop(SIDE + LAG, 2 * SIDE + LAG, both, 0, unroll=2)
    send_group(1)
    lax.fori_loop(2 * SIDE + LAG, 3 * SIDE + LAG, both, 0, unroll=2)
    send_group(2)
    lax.fori_loop(3 * SIDE + LAG, total, both, 0, unroll=2)
    lax.fori_loop(total - LAG, total, final, 0, unroll=2)
    send_group(3)

    for g in range(2):
        row_done(0, g)
        row_done(2, g)
    for d in NEAR_FIRST:
        stage1[1, d].wait_recv()
    for d in NEAR_FIRST:
        add_row(1, lax.rem(where[2] + d, SIDE))
        send2(1, d)
    add_row(1, where[2])
    row_done(0, 2)
    row_done(2, 2)
    send3(1)
    row_done(0, 3)
    send3(0)
    row_done(2, 3)
    send3(2)
    for p in (1, 0, 2):
        lo, hi, order = PARTS[p]
        v = s3[p][where[order[2]]]
        for d in range(1, SIDE):
            stage3[p, d].wait_recv()
            v = v + r3[p][d - 1]
        units[lo:hi] = v

    for k in range(2):
        for lg in range(2):
            for rh in range(2):
                ur = k * 8 + lg * 2 + rh
                re = units[ur]
                im = units[ur + 4]
                power = re * re + im * im
                wf[(core,) + where + (ur,)] = (re * power).astype(jnp.bfloat16)
                wf[(core,) + where + (ur + 4,)] = (im * power).astype(jnp.bfloat16)
                rows = slice(rh * SUB, (rh + 1) * SUB)
                scene_ref[k, rows, lg * LANE : (lg + 1) * LANE] = re
                scene_ref[k, rows, (lg + 2) * LANE : (lg + 3) * LANE] = im

    gathers = {}

    def gather(p, fixed, axis, d, key, step):
        lo, hi, _ = GATHER_PARTS[p]
        src = wf.at[(core,) + pick(fixed, lo, hi)]
        n = len(gathers)
        cp = pltpu.make_async_remote_copy(
            src_ref=src,
            dst_ref=src,
            send_sem=gsend.at[step],
            recv_sem=grecv.at[n],
            device_id=device_at(shifted(where, axis, d), core),
            device_id_type=MESH,
        )
        cp.start()
        gathers[key] = cp

    def forward(p, fixed):
        lo, hi, _ = GATHER_PARTS[p]
        src = wf.at[(core,) + pick(fixed, lo, hi)]
        cp = pltpu.make_async_remote_copy(
            src_ref=src,
            dst_ref=src,
            send_sem=fsend.at[0],
            recv_sem=frecv.at[0],
            device_id=other,
            device_id_type=MESH,
        )
        cp.start()

    def back(axis, d):
        return lax.rem(where[axis] + SIDE - d, SIDE)

    order_of = (2, 0, 1)
    for p in order_of:
        for d in NEAR_FIRST:
            gather(p, dict(enumerate(where)), GATHER_PARTS[p][2][2], d, (p, "c", d), 0)

    def row_out(p, r):
        a, b, c = GATHER_PARTS[p][2]
        row = {a: where[a], b: back(b, r)}
        for d in NEAR_FIRST if r == LAST_ROW else (1, 3):
            gather(p, row, a, d, (p, r, d), 2)
        forward(p, row)

    for p in order_of:
        a, b, c = GATHER_PARTS[p][2]
        for d in NEAR_FIRST:
            gathers[p, "c", d].wait_recv()
        for d in NEAR_FIRST:
            gather(p, {a: where[a], b: where[b]}, b, d, (p, "b", d), 1)
        row_out(p, 0)
    for d in NEAR_FIRST:
        for p in order_of:
            gathers[p, "b", d].wait_recv()
            row_out(p, d)
    for r in (0, 1, 3):
        for p in order_of:
            a, b, c = GATHER_PARTS[p][2]
            for d, half in ((1, slice(0, 2)), (3, slice(2, 4))):
                gathers[p, r, d].wait_recv()
                gather(p, {a: back(a, d), b: back(b, r), c: half}, a, d, (p, r, "far", d), 2)
                forward(p, {a: back(a, d), b: back(b, r)})
    for r in (0, 1, 3):
        for p in order_of:
            a, b, c = GATHER_PARTS[p][2]
            for d in (1, 3):
                gathers[p, r, "far", d].wait_recv()
            forward(p, {a: back(a, 2), b: back(b, r)})
    for d in NEAR_FIRST:
        for p in order_of:
            a, b, c = GATHER_PARTS[p][2]
            gathers[p, LAST_ROW, d].wait_recv()
            forward(p, {a: back(a, d), b: back(b, LAST_ROW)})
    pltpu.make_async_copy(wf.at[1 - core], wf.at[1 - core], frecv.at[0]).wait()

    acc[...] = jnp.zeros_like(acc)

    def backward(j, carry):
        zj = plan_ref[2, j]
        xj = plan_ref[3, j]
        kj = plan_ref[4, j]
        live = jnp.where(plan_ref[5, j] > 0, jnp.float32(1.0), jnp.float32(0.0))
        groups = []
        for lg in range(4):
            pieces = [
                wf[((c,) + ((y, zj, xj) if c == 0 else (xj, zj, y))) + (pl.ds(kj * 8 + lg * 2, 2),)].reshape(2 * SUB, LANE)
                for y in range(SIDE)
                for c in range(2)
            ]
            groups.append(jnp.concatenate(pieces, axis=0))
        weight = jnp.concatenate(groups, axis=1)
        moments = lax.dot_general(
            weight, stacked[kj], (((1,), (1,)), ((), ())), preferred_element_type=jnp.float32
        )
        re = steer[j, :, :pulses].astype(jnp.float32)
        im = steer[j, :, pulses:].astype(jnp.float32)
        term = im * moments[:, :pulses] - re * moments[:, pulses:]
        acc[...] += jnp.sum(term.reshape(-1, 8, pulses), axis=0) * live
        return carry

    lax.fori_loop(0, slots, backward, 0, unroll=4)
    factor = -4.0 / math.sqrt(steer.shape[1] * (stacked.shape[2] // 2))
    grad_ref[...] = jnp.sum(acc[...], axis=0, keepdims=True) * factor

    def all_sent(like, sem):
        pltpu.make_async_copy(like, like, sem).wait()

    all_sent(crecv, csend.at[0])
    all_sent(s1.at[:3], s1send.at[0])
    all_sent(s1.at[0, :3], s2send.at[0])
    for p in range(3):
        all_sent(r3[p], s3send.at[p])
    all_sent(wf.at[0, 0, 0, :3], gsend.at[0])
    all_sent(wf.at[0, 0, :3], gsend.at[1])
    all_sent(wf.at[0, :3], gsend.at[2])
    all_sent(wf.at[core], fsend.at[0])


def on_device(echoes, phases, kernel, steering, footprint, counts, range_start):
    columns = lax.axis_size("tile")
    row_parts = lax.axis_size("pulse")
    pulses = echoes.shape[0]
    breadth = kernel.shape[2]
    height = steering.shape[2]
    slots = steering.shape[1]
    tile_rows = range_start.shape[1]
    part_rows = height // row_parts
    width = 2 * breadth

    f32, bf16 = jnp.float32, jnp.bfloat16
    sizes = [hi - lo for lo, hi, _ in PARTS]
    vmem = pltpu.VMEM
    sem = lambda n: pltpu.SemaphoreType.DMA((n,))
    anywhere = pl.BlockSpec(memory_space=pl.ANY)
    smem = pl.BlockSpec(memory_space=pltpu.SMEM)
    whole = pl.BlockSpec(memory_space=pltpu.VMEM)
    span = kernel.shape[1] + LANE
    plan, mask, trig, stacked = pl.pallas_call(
        local_kernel,
        out_shape=(
            jax.ShapeDtypeStruct((6, columns), jnp.int32),
            jax.ShapeDtypeStruct((columns * tile_rows, LANE), f32),
            jax.ShapeDtypeStruct((2, pulses), f32),
            jax.ShapeDtypeStruct((tile_rows, 2 * pulses, width), bf16),
        ),
        in_specs=[smem] * 3 + [whole] * 2 + [anywhere],
        out_specs=[smem] + [whole] * 2 + [anywhere],
        scratch_shapes=[
            vmem((tile_rows, 2 * pulses, width), bf16),
            vmem((tile_rows, pulses, 2, span), bf16),
            vmem((SIDE, breadth // LANE, 2 * pulses // SIDE, LANE), f32),
            sem(4),
        ],
    )(footprint, counts, range_start, phases[None], kernel[0], echoes)
    scene, grad = pl.pallas_call(
        main_kernel,
        out_shape=(
            jax.ShapeDtypeStruct((tile_rows, part_rows, width), f32),
            jax.ShapeDtypeStruct((1, pulses), f32),
        ),
        in_specs=[smem] + [anywhere] * 4,
        out_specs=[whole] * 2,
        scratch_shapes=[
            vmem((columns * tile_rows, LANE), f32),
            vmem((columns * tile_rows, LANE), f32),
            vmem((2, pulses), f32),
            vmem((tile_rows, 2 * pulses, width), bf16),
            vmem((slots, height, 2 * pulses), bf16),
            vmem((columns, SIDE, 2, part_rows, width), f32),
            vmem((columns, SIDE, part_rows, width), f32),
            vmem((SIDE, SIDE, SIDE, 16, SUB, LANE), bf16),
        ]
        + [vmem((3, SIDE, SIDE, n, SUB, LANE), bf16) for n in sizes]
        + [vmem((SIDE, SIDE, n, SUB, LANE), bf16) for n in sizes]
        + [vmem((3, SIDE, n, SUB, LANE), bf16) for n in sizes]
        + [vmem((SIDE, n, SUB, LANE), f32) for n in sizes]
        + [vmem((3, n, SUB, LANE), f32) for n in sizes]
        + [
            vmem((16, SUB, LANE), f32),
            vmem((2, SIDE, SIDE, SIDE, 16, SUB, LANE), bf16),
            vmem((8, pulses), f32),
            sem(slots + 3),
            sem(2),
            sem(1), sem(columns),
            sem(1), sem(27),
            sem(1), sem(9),
            sem(3), sem(9),
            sem(3), sem(66),
            sem(1), sem(1),
        ],
        compiler_params=pltpu.CompilerParams(
            collective_id=0, has_side_effects=True, vmem_limit_bytes=60 << 20
        ),
    )(plan, mask, trig, stacked, steering[0])
    return (scene[:, None], grad[0])


def solution(mesh):
    placed = (
        P(("pulse", "tile"), None, None),
        P(("pulse", "tile")),
        P(("pulse", "tile"), None, None),
        P(("pulse", "tile"), None, None, None),
        P(("pulse", "tile"), None),
        P(("pulse", "tile")),
        P(("pulse", "tile"), None),
    )
    return jax.shard_map(
        on_device,
        mesh=mesh,
        in_specs=placed,
        out_specs=(P(None, "tile", "pulse", None), P(("pulse", "tile"))),
        check_vma=False,
    )
```

```python
import functools
import math

import jax
import jax.numpy as jnp
from jax import lax
from jax.experimental import pallas as pl
from jax.experimental.pallas import tpu as pltpu
from jax.sharding import PartitionSpec as P

MESH = pl.DeviceIdType.MESH
SIDE = 4
LANE = 128
SUB = 16
PARTS = (
    (0, 6, (0, 1, 2)),
    (6, 10, (1, 2, 0)),
    (10, 16, (2, 1, 0)),
)
GATHER_PARTS = (
    (0, 5, (0, 1, 2)),
    (5, 10, (1, 2, 0)),
    (10, 16, (2, 0, 1)),
)
NEAR_FIRST = (1, 3, 2)
LAST_ROW = 2
LAG = 2


def position():
    p = lax.axis_index("pulse")
    t = lax.axis_index("tile")
    core = p % 2
    return turned((p // 2, t // SIDE, t % SIDE), core), core


def turned(place, core):
    first = jnp.where(core == 0, place[0], place[2])
    last = jnp.where(core == 0, place[2], place[0])
    return (first, place[1], last)


def device_at(where, core):
    y, z, x = turned(where, core)
    return (y * 2 + core, z * SIDE + x)


def shifted(where, axis, d):
    moved = list(where)
    moved[axis] = lax.rem(where[axis] + d, SIDE)
    return tuple(moved)


def pick(fixed, lo, hi):
    return tuple(fixed.get(a, slice(None)) for a in range(3)) + (slice(lo, hi),)


def local_kernel(
    foot_ref,
    count_ref,
    start_ref,
    phases_ref,
    kernel_ref,
    echoes_in,
    plan_ref,
    mask,
    trig,
    stacked_out,
    stacked,
    windows,
    raw,
    sem,
):
    pulses = phases_ref.shape[1]
    window_len, breadth = kernel_ref.shape
    span = window_len + LANE
    last = (echoes_in.shape[2] - span) // LANE
    slots = foot_ref.shape[1]
    blocks = [jnp.minimum(start_ref[0, k] // LANE, last) for k in range(2)]
    copies, outs = [], []
    for k in range(2):
        cp = pltpu.make_async_copy(
            echoes_in.at[:, :, pl.ds(pl.multiple_of(blocks[k] * LANE, LANE), span)], windows.at[k], sem.at[k]
        )
        cp.start()
        copies.append(cp)
    count = count_ref[0]
    for t in range(SIDE * SIDE):
        for n in range(6):
            plan_ref[n, t] = jnp.int32(0)
    tile_id = lax.broadcasted_iota(jnp.int32, mask.shape, 0)
    tile_id = tile_id // 2 + tile_id % 2 * (SIDE * SIDE)
    found = jnp.zeros(mask.shape, jnp.float32)
    for j in range(slots):
        name = foot_ref[0, j]
        live = j < count
        found = jnp.where(tile_id == jnp.where(live, name, -1), jnp.float32(1.0), found)
        plan_ref[2, j] = name // SIDE % SIDE
        plan_ref[3, j] = name % SIDE
        plan_ref[4, j] = name // (SIDE * SIDE)
        plan_ref[5, j] = live.astype(jnp.int32)

        @pl.when(live)
        def _():
            t = name % (SIDE * SIDE)
            plan_ref[0, t] = jnp.int32(j)
            plan_ref[1, t] = name // (SIDE * SIDE)

    mask[...] = found
    angle = phases_ref[...]
    trig[0:1, :] = jnp.cos(angle)
    trig[1:2, :] = jnp.sin(angle)
    depth = pulses // SIDE
    for k in range(2):
        weights = jnp.concatenate(
            [kernel_ref[...].astype(jnp.float32), jnp.zeros((LANE, breadth), jnp.float32)], axis=0
        )
        weights = pltpu.roll(weights, start_ref[0, k] - blocks[k] * LANE, 0).astype(jnp.bfloat16)
        copies[k].wait()

        for i in range(SIDE):
            at = i * depth
            window = windows[k, pl.ds(at, depth)]
            value = jnp.dot(window.reshape(2 * depth, span), weights, preferred_element_type=jnp.float32)
            top, low = pl.ds(at, depth), pl.ds(pulses + at, depth)
            for h in range(breadth // LANE):
                raw[i, h] = value[:, h * LANE : (h + 1) * LANE]
                re = raw[i, h, pl.ds(0, depth, stride=2), :].astype(jnp.bfloat16)
                im = raw[i, h, pl.ds(1, depth, stride=2), :].astype(jnp.bfloat16)
                left = slice(h * LANE, (h + 1) * LANE)
                right = slice(breadth + h * LANE, breadth + (h + 1) * LANE)
                stacked[k, top, left] = re
                stacked[k, top, right] = im
                stacked[k, low, left] = -im
                stacked[k, low, right] = re
        out = pltpu.make_async_copy(stacked.at[k], stacked_out.at[k], sem.at[2 + k])
        out.start()
        outs.append(out)
    for out in outs:
        out.wait()


def hand_on(scene_in, grad_in, scene_out, grad_out):
    scene_out[...] = scene_in[...]
    grad_out[...] = jnp.sum(grad_in[...], axis=0, keepdims=True)


def main_kernel(
    plan_ref,
    mask_in,
    trig_in,
    stacked_in,
    steer_in,
    scene_out,
    grad_ref,
    scene_ref,
    mask,
    omask,
    trig,
    stacked,
    steer,
    tiles,
    crecv,
    s1,
    r1a, r1b, r1c,
    s2a, s2b, s2c,
    r2a, r2b, r2c,
    s3a, s3b, s3c,
    r3a, r3b, r3c,
    units,
    wf,
    acc,
    lsem,
    msem,
    csend, crcv,
    s1send, s1recv,
    s2send, s2recv,
    s3send, s3recv,
    gsend, grecv,
    fsend, frecv,
):
    r1, s2, r2, s3, r3 = (r1a, r1b, r1c), (s2a, s2b, s2c), (r2a, r2b, r2c), (s3a, s3b, s3c), (r3a, r3b, r3c)
    where, core = position()
    y_own, z_own, x_own = turned(where, core)
    other = (y_own * 2 + 1 - core, z_own * SIDE + x_own)
    pulses = trig.shape[1]
    slots = steer.shape[0]

    for j in range(slots):
        pltpu.make_async_copy(steer_in.at[j], steer.at[j], lsem.at[j]).start()
    local = []
    for n, (src, dst) in enumerate(((mask_in, mask), (trig_in, trig), (stacked_in, stacked))):
        cp = pltpu.make_async_copy(src, dst, lsem.at[slots + n])
        cp.start()
        local.append(cp)

    barrier = pltpu.get_barrier_semaphore()
    pl.semaphore_signal(barrier, inc=1, device_id=other, device_id_type=MESH)
    for axis in range(3):
        for d in range(1, SIDE):
            pl.semaphore_signal(
                barrier, inc=1, device_id=device_at(shifted(where, axis, d), core), device_id_type=MESH
            )
    local[0].wait()
    local[1].wait()

    def turn(j, carry):
        pltpu.make_async_copy(steer_in.at[j], steer.at[j], lsem.at[j]).wait()
        cosine = trig[0:1, :]
        sines = trig[1:2, :]

        def rows(i, c2):
            at = pl.ds(pl.multiple_of(i * 64, 64), 64)
            re = steer[j, at, :pulses].astype(jnp.float32)
            im = steer[j, at, pulses:].astype(jnp.float32)
            steer[j, at, :pulses] = (re * cosine - im * sines).astype(jnp.bfloat16)
            steer[j, at, pulses:] = (re * sines + im * cosine).astype(jnp.bfloat16)
            return c2

        return lax.fori_loop(0, steer.shape[1] // 64, rows, carry)

    lax.fori_loop(0, slots, turn, 0)

    pl.semaphore_wait(barrier, 10)
    mcopy = pltpu.make_async_remote_copy(
        src_ref=mask, dst_ref=omask, send_sem=msem.at[0], recv_sem=msem.at[1], device_id=other, device_id_type=MESH
    )
    mcopy.start()
    local[2].wait()

    def core_copy(t):
        return pltpu.make_async_remote_copy(
            src_ref=tiles.at[t, :, 1 - core],
            dst_ref=crecv.at[t],
            send_sem=csend.at[0],
            recv_sem=crcv.at[t],
            device_id=other,
            device_id_type=MESH,
        )

    stage1, stage2, stage3 = {}, {}, {}

    def send1(p, d, src_fixed, key):
        lo, hi, order = PARTS[p]
        axis = order[0]
        fixed = dict(src_fixed)
        target = shifted(where, axis, d)
        fixed[axis] = target[axis]
        dst = tuple(src_fixed.get(a, slice(None)) for a in range(3) if a != axis)
        n = len(stage1)
        cp = pltpu.make_async_remote_copy(
            src_ref=s1.at[pick(fixed, lo, hi)],
            dst_ref=r1[p].at[(d - 1,) + dst],
            send_sem=s1send.at[0],
            recv_sem=s1recv.at[n],
            device_id=device_at(target, core),
            device_id_type=MESH,
        )
        cp.start()
        stage1[key] = cp

    def rest_index(p, fixed):
        return tuple(fixed.get(a, slice(None)) for a in range(3) if a != PARTS[p][2][0])

    def add_row(p, row):
        lo, hi, (a, b, c) = PARTS[p]

        def add(o, carry):
            here = rest_index(p, {b: row, c: o})
            v = s1[pick({a: where[a], b: row, c: o}, lo, hi)].astype(jnp.float32)
            for d in range(SIDE - 1):
                v = v + r1[p][(d,) + here].astype(jnp.float32)
            s2[p][here] = v.astype(jnp.bfloat16)
            return carry

        lax.fori_loop(0, SIDE, add, 0, unroll=True)

    def send2(p, d):
        b = PARTS[p][2][1]
        target = shifted(where, b, d)
        cp = pltpu.make_async_remote_copy(
            src_ref=s2[p].at[rest_index(p, {b: target[b]})],
            dst_ref=r2[p].at[d - 1],
            send_sem=s2send.at[0],
            recv_sem=s2recv.at[p * 3 + d - 1],
            device_id=device_at(target, core),
            device_id_type=MESH,
        )
        cp.start()
        stage2[p, d] = cp

    def row_done(p, g):
        for d in NEAR_FIRST:
            stage1[p, g, d].wait_recv()
        add_row(p, lax.rem(where[1] + 1 + g, SIDE))
        if g < SIDE - 1:
            send2(p, g + 1)

    def send3(p):
        lo, hi, (a, b, c) = PARTS[p]
        for d in NEAR_FIRST:
            stage2[p, d].wait_recv()
        for q in range(SIDE):
            v = s2[p][rest_index(p, {b: where[b], c: q})].astype(jnp.float32)
            for d in range(SIDE - 1):
                v = v + r2[p][d, q].astype(jnp.float32)
            s3[p][q] = v
        for d in NEAR_FIRST:
            target = shifted(where, c, d)
            cp = pltpu.make_async_remote_copy(
                src_ref=s3[p].at[target[c]],
                dst_ref=r3[p].at[d - 1],
                send_sem=s3send.at[p],
                recv_sem=s3recv.at[p * 3 + d - 1],
                device_id=device_at(target, core),
                device_id_type=MESH,
            )
            cp.start()
            stage3[p, d] = cp

    def column(i):
        return lax.rem(where[1] + 1 + i // SIDE, SIDE), i % SIDE

    def compute(i):
        z, x = column(i)
        t = z * SIDE + x
        left = steer[plan_ref[0, t]]
        right = stacked[plan_ref[1, t]]
        part = jnp.dot(left, right, preferred_element_type=jnp.float32)
        tiles[t] = part.reshape(tiles.shape[1:])
        core_copy(t).start()

    def combine(i):
        z, x = column(i)
        t = z * SIDE + x
        core_copy(t).wait_recv()
        for k in range(2):
            m = mask[pl.ds(t * 2 + k, 1), :]
            om = omask[pl.ds(t * 2 + k, 1), :]
            for lg in range(4):
                lanes = slice(lg * LANE, (lg + 1) * LANE)
                for y in range(SIDE):
                    v = tiles[t, y, core, :, lanes] * m + crecv[t, y, :, lanes] * om
                    u = k * 8 + lg * 2
                    s1[turned((y, z, x), core) + (slice(u, u + 2),)] = v.astype(jnp.bfloat16).reshape(2, SUB, LANE)

    def send_group(g):
        z = lax.rem(where[1] + 1 + g, SIDE)
        for d in NEAR_FIRST:
            send1(0, d, {1: z}, (0, g, d))
            send1(2, d, {1: z}, (2, g, d))
        if g < SIDE - 1:
            send1(1, g + 1, {}, (1, g + 1))

    def both(i, carry):
        compute(i)
        combine(i - LAG)
        return carry

    def first(i, carry):
        compute(i)
        return carry

    def final(i, carry):
        combine(i)
        return carry

    total = SIDE * SIDE
    lax.fori_loop(0, LAG, first, 0, unroll=2)
    mcopy.wait()
    lax.fori_loop(LAG, SIDE + LAG, both, 0, unroll=2)
    send_group(0)
    lax.fori_loop(SIDE + LAG, 2 * SIDE + LAG, both, 0, unroll=2)
    send_group(1)
    lax.fori_loop(2 * SIDE + LAG, 3 * SIDE + LAG, both, 0, unroll=2)
    send_group(2)
    lax.fori_loop(3 * SIDE + LAG, total, both, 0, unroll=2)
    lax.fori_loop(total - LAG, total, final, 0, unroll=2)
    send_group(3)

    for g in range(2):
        row_done(0, g)
        row_done(2, g)
    for d in NEAR_FIRST:
        stage1[1, d].wait_recv()
    for d in NEAR_FIRST:
        add_row(1, lax.rem(where[2] + d, SIDE))
        send2(1, d)
    add_row(1, where[2])
    row_done(0, 2)
    row_done(2, 2)
    send3(1)
    row_done(0, 3)
    send3(0)
    row_done(2, 3)
    send3(2)
    for p in (1, 0, 2):
        lo, hi, order = PARTS[p]
        v = s3[p][where[order[2]]]
        for d in range(1, SIDE):
            stage3[p, d].wait_recv()
            v = v + r3[p][d - 1]
        units[lo:hi] = v

    for k in range(2):
        for lg in range(2):
            for rh in range(2):
                ur = k * 8 + lg * 2 + rh
                re = units[ur]
                im = units[ur + 4]
                power = re * re + im * im
                wf[(core,) + where + (ur,)] = (re * power).astype(jnp.bfloat16)
                wf[(core,) + where + (ur + 4,)] = (im * power).astype(jnp.bfloat16)
                rows = slice(rh * SUB, (rh + 1) * SUB)
                scene_ref[k, rows, lg * LANE : (lg + 1) * LANE] = re
                scene_ref[k, rows, (lg + 2) * LANE : (lg + 3) * LANE] = im

    scene_copy = pltpu.make_async_copy(scene_ref, scene_out, lsem.at[0])
    scene_copy.start()

    gathers = {}

    def gather(p, fixed, axis, d, key, step):
        lo, hi, _ = GATHER_PARTS[p]
        src = wf.at[(core,) + pick(fixed, lo, hi)]
        n = len(gathers)
        cp = pltpu.make_async_remote_copy(
            src_ref=src,
            dst_ref=src,
            send_sem=gsend.at[step],
            recv_sem=grecv.at[n],
            device_id=device_at(shifted(where, axis, d), core),
            device_id_type=MESH,
        )
        cp.start()
        gathers[key] = cp

    def forward(p, fixed):
        lo, hi, _ = GATHER_PARTS[p]
        src = wf.at[(core,) + pick(fixed, lo, hi)]
        cp = pltpu.make_async_remote_copy(
            src_ref=src,
            dst_ref=src,
            send_sem=fsend.at[0],
            recv_sem=frecv.at[0],
            device_id=other,
            device_id_type=MESH,
        )
        cp.start()

    def back(axis, d):
        return lax.rem(where[axis] + SIDE - d, SIDE)

    order_of = (2, 0, 1)
    for p in order_of:
        for d in NEAR_FIRST:
            gather(p, dict(enumerate(where)), GATHER_PARTS[p][2][2], d, (p, "c", d), 0)

    def row_out(p, r):
        a, b, c = GATHER_PARTS[p][2]
        row = {a: where[a], b: back(b, r)}
        for d in NEAR_FIRST if r == LAST_ROW else (1, 3):
            gather(p, row, a, d, (p, r, d), 2)
        forward(p, row)

    for p in order_of:
        a, b, c = GATHER_PARTS[p][2]
        for d in NEAR_FIRST:
            gathers[p, "c", d].wait_recv()
        for d in NEAR_FIRST:
            gather(p, {a: where[a], b: where[b]}, b, d, (p, "b", d), 1)
        row_out(p, 0)
    for d in NEAR_FIRST:
        for p in order_of:
            gathers[p, "b", d].wait_recv()
            row_out(p, d)
    for r in (0, 1, 3):
        for p in order_of:
            a, b, c = GATHER_PARTS[p][2]
            for d, half in ((1, slice(0, 2)), (3, slice(2, 4))):
                gathers[p, r, d].wait_recv()
                gather(p, {a: back(a, d), b: back(b, r), c: half}, a, d, (p, r, "far", d), 2)
                forward(p, {a: back(a, d), b: back(b, r)})
    for r in (0, 1, 3):
        for p in order_of:
            a, b, c = GATHER_PARTS[p][2]
            for d in (1, 3):
                gathers[p, r, "far", d].wait_recv()
            forward(p, {a: back(a, 2), b: back(b, r)})
    for d in NEAR_FIRST:
        for p in order_of:
            a, b, c = GATHER_PARTS[p][2]
            gathers[p, LAST_ROW, d].wait_recv()
            forward(p, {a: back(a, d), b: back(b, LAST_ROW)})
    pltpu.make_async_copy(wf.at[1 - core], wf.at[1 - core], frecv.at[0]).wait()

    acc[...] = jnp.zeros_like(acc)

    def backward(j, carry):
        zj = plan_ref[2, j]
        xj = plan_ref[3, j]
        kj = plan_ref[4, j]
        live = jnp.where(plan_ref[5, j] > 0, jnp.float32(1.0), jnp.float32(0.0))
        groups = []
        for lg in range(4):
            pieces = [
                wf[((c,) + ((y, zj, xj) if c == 0 else (xj, zj, y))) + (pl.ds(kj * 8 + lg * 2, 2),)].reshape(2 * SUB, LANE)
                for y in range(SIDE)
                for c in range(2)
            ]
            groups.append(jnp.concatenate(pieces, axis=0))
        weight = jnp.concatenate(groups, axis=1)
        moments = lax.dot_general(
            weight, stacked[kj], (((1,), (1,)), ((), ())), preferred_element_type=jnp.float32
        )
        re = steer[j, :, :pulses].astype(jnp.float32)
        im = steer[j, :, pulses:].astype(jnp.float32)
        term = im * moments[:, :pulses] - re * moments[:, pulses:]
        acc[...] += jnp.sum(term.reshape(-1, 8, pulses), axis=0) * live
        return carry

    lax.fori_loop(0, slots, backward, 0, unroll=4)
    factor = -4.0 / math.sqrt(steer.shape[1] * (stacked.shape[2] // 2))
    grad_ref[...] = acc[...] * factor

    scene_copy.wait()
    def all_sent(like, sem):
        pltpu.make_async_copy(like, like, sem).wait()

    all_sent(crecv, csend.at[0])
    all_sent(s1.at[:3], s1send.at[0])
    all_sent(s1.at[0, :3], s2send.at[0])
    for p in range(3):
        all_sent(r3[p], s3send.at[p])
    all_sent(wf.at[0, 0, 0, :3], gsend.at[0])
    all_sent(wf.at[0, 0, :3], gsend.at[1])
    all_sent(wf.at[0, :3], gsend.at[2])
    all_sent(wf.at[core], fsend.at[0])


def on_device(echoes, phases, kernel, steering, footprint, counts, range_start):
    columns = lax.axis_size("tile")
    row_parts = lax.axis_size("pulse")
    pulses = echoes.shape[0]
    breadth = kernel.shape[2]
    height = steering.shape[2]
    slots = steering.shape[1]
    tile_rows = range_start.shape[1]
    part_rows = height // row_parts
    width = 2 * breadth

    f32, bf16 = jnp.float32, jnp.bfloat16
    sizes = [hi - lo for lo, hi, _ in PARTS]
    vmem = pltpu.VMEM
    sem = lambda n: pltpu.SemaphoreType.DMA((n,))
    anywhere = pl.BlockSpec(memory_space=pl.ANY)
    smem = pl.BlockSpec(memory_space=pltpu.SMEM)
    whole = pl.BlockSpec(memory_space=pltpu.VMEM)
    span = kernel.shape[1] + LANE
    plan, mask, trig, stacked = pl.pallas_call(
        local_kernel,
        out_shape=(
            jax.ShapeDtypeStruct((6, columns), jnp.int32),
            jax.ShapeDtypeStruct((columns * tile_rows, LANE), f32),
            jax.ShapeDtypeStruct((2, pulses), f32),
            jax.ShapeDtypeStruct((tile_rows, 2 * pulses, width), bf16),
        ),
        in_specs=[smem] * 3 + [whole] * 2 + [anywhere],
        out_specs=[smem] + [whole] * 2 + [anywhere],
        scratch_shapes=[
            vmem((tile_rows, 2 * pulses, width), bf16),
            vmem((tile_rows, pulses, 2, span), bf16),
            vmem((SIDE, breadth // LANE, 2 * pulses // SIDE, LANE), f32),
            sem(4),
        ],
    )(footprint, counts, range_start, phases[None], kernel[0], echoes)
    scene, grad = pl.pallas_call(
        main_kernel,
        out_shape=(
            jax.ShapeDtypeStruct((tile_rows, part_rows, width), f32),
            jax.ShapeDtypeStruct((8, pulses), f32),
        ),
        in_specs=[smem] + [anywhere] * 4,
        out_specs=[anywhere, whole],
        scratch_shapes=[
            vmem((tile_rows, part_rows, width), f32),
            vmem((columns * tile_rows, LANE), f32),
            vmem((columns * tile_rows, LANE), f32),
            vmem((2, pulses), f32),
            vmem((tile_rows, 2 * pulses, width), bf16),
            vmem((slots, height, 2 * pulses), bf16),
            vmem((columns, SIDE, 2, part_rows, width), f32),
            vmem((columns, SIDE, part_rows, width), f32),
            vmem((SIDE, SIDE, SIDE, 16, SUB, LANE), bf16),
        ]
        + [vmem((3, SIDE, SIDE, n, SUB, LANE), bf16) for n in sizes]
        + [vmem((SIDE, SIDE, n, SUB, LANE), bf16) for n in sizes]
        + [vmem((3, SIDE, n, SUB, LANE), bf16) for n in sizes]
        + [vmem((SIDE, n, SUB, LANE), f32) for n in sizes]
        + [vmem((3, n, SUB, LANE), f32) for n in sizes]
        + [
            vmem((16, SUB, LANE), f32),
            vmem((2, SIDE, SIDE, SIDE, 16, SUB, LANE), bf16),
            vmem((8, pulses), f32),
            sem(slots + 3),
            sem(2),
            sem(1), sem(columns),
            sem(1), sem(27),
            sem(1), sem(9),
            sem(3), sem(9),
            sem(3), sem(66),
            sem(1), sem(1),
        ],
        compiler_params=pltpu.CompilerParams(
            collective_id=0, has_side_effects=True, vmem_limit_bytes=60 << 20
        ),
    )(plan, mask, trig, stacked, steering[0])
    scene, grad = pl.pallas_call(
        hand_on,
        out_shape=(
            jax.ShapeDtypeStruct(scene.shape, f32),
            jax.ShapeDtypeStruct((1, pulses), f32),
        ),
        in_specs=[whole] * 2,
        out_specs=[whole] * 2,
    )(scene, grad)
    return (scene[:, None], grad[0])


def solution(mesh):
    placed = (
        P(("pulse", "tile"), None, None),
        P(("pulse", "tile")),
        P(("pulse", "tile"), None, None),
        P(("pulse", "tile"), None, None, None),
        P(("pulse", "tile"), None),
        P(("pulse", "tile")),
        P(("pulse", "tile"), None),
    )
    return jax.shard_map(
        on_device,
        mesh=mesh,
        in_specs=placed,
        out_specs=(P(None, "tile", "pulse", None), P(("pulse", "tile"))),
        check_vma=False,
    )
```

```python
import functools
import math

import jax
import jax.numpy as jnp
from jax import lax
from jax.experimental import pallas as pl
from jax.experimental.pallas import tpu as pltpu
from jax.sharding import PartitionSpec as P

MESH = pl.DeviceIdType.MESH
SIDE = 4
LANE = 128
SUB = 16
PARTS = (
    (0, 6, (0, 1, 2)),
    (6, 10, (1, 2, 0)),
    (10, 16, (2, 1, 0)),
)
GATHER_PARTS = (
    (0, 5, (0, 1, 2)),
    (5, 10, (1, 2, 0)),
    (10, 16, (2, 0, 1)),
)
NEAR_FIRST = (1, 3, 2)
LAST_ROW = 2
LAG = 2


def position():
    p = lax.axis_index("pulse")
    t = lax.axis_index("tile")
    core = p % 2
    return turned((p // 2, t // SIDE, t % SIDE), core), core


def turned(place, core):
    first = jnp.where(core == 0, place[0], place[2])
    last = jnp.where(core == 0, place[2], place[0])
    return (first, place[1], last)


def device_at(where, core):
    y, z, x = turned(where, core)
    return (y * 2 + core, z * SIDE + x)


def shifted(where, axis, d):
    moved = list(where)
    moved[axis] = lax.rem(where[axis] + d, SIDE)
    return tuple(moved)


def pick(fixed, lo, hi):
    return tuple(fixed.get(a, slice(None)) for a in range(3)) + (slice(lo, hi),)


def local_kernel(
    foot_ref,
    count_ref,
    start_ref,
    phases_ref,
    kernel_ref,
    echoes_in,
    plan_ref,
    mask,
    trig,
    stacked_out,
    stacked,
    windows,
    raw,
    sem,
):
    pulses = phases_ref.shape[1]
    window_len, breadth = kernel_ref.shape
    span = window_len + LANE
    last = (echoes_in.shape[2] - span) // LANE
    slots = foot_ref.shape[1]
    blocks = [jnp.minimum(start_ref[0, k] // LANE, last) for k in range(2)]
    copies, outs = [], []
    for k in range(2):
        cp = pltpu.make_async_copy(
            echoes_in.at[:, :, pl.ds(pl.multiple_of(blocks[k] * LANE, LANE), span)], windows.at[k], sem.at[k]
        )
        cp.start()
        copies.append(cp)
    count = count_ref[0]
    for t in range(SIDE * SIDE):
        for n in range(6):
            plan_ref[n, t] = jnp.int32(0)
    tile_id = lax.broadcasted_iota(jnp.int32, mask.shape, 0)
    tile_id = tile_id // 2 + tile_id % 2 * (SIDE * SIDE)
    found = jnp.zeros(mask.shape, jnp.float32)
    for j in range(slots):
        name = foot_ref[0, j]
        live = j < count
        found = jnp.where(tile_id == jnp.where(live, name, -1), jnp.float32(1.0), found)
        plan_ref[2, j] = name // SIDE % SIDE
        plan_ref[3, j] = name % SIDE
        plan_ref[4, j] = name // (SIDE * SIDE)
        plan_ref[5, j] = live.astype(jnp.int32)

        @pl.when(live)
        def _():
            t = name % (SIDE * SIDE)
            plan_ref[0, t] = jnp.int32(j)
            plan_ref[1, t] = name // (SIDE * SIDE)

    mask[...] = found
    angle = phases_ref[...]
    trig[0:1, :] = jnp.cos(angle)
    trig[1:2, :] = jnp.sin(angle)
    depth = pulses // SIDE
    for k in range(2):
        weights = jnp.concatenate(
            [kernel_ref[...].astype(jnp.float32), jnp.zeros((LANE, breadth), jnp.float32)], axis=0
        )
        weights = pltpu.roll(weights, start_ref[0, k] - blocks[k] * LANE, 0).astype(jnp.bfloat16)
        copies[k].wait()

        for i in range(SIDE):
            at = i * depth
            window = windows[k, pl.ds(at, depth)]
            value = jnp.dot(window.reshape(2 * depth, span), weights, preferred_element_type=jnp.float32)
            top, low = pl.ds(at, depth), pl.ds(pulses + at, depth)
            for h in range(breadth // LANE):
                raw[i, h] = value[:, h * LANE : (h + 1) * LANE]
                re = raw[i, h, pl.ds(0, depth, stride=2), :].astype(jnp.bfloat16)
                im = raw[i, h, pl.ds(1, depth, stride=2), :].astype(jnp.bfloat16)
                left = slice(h * LANE, (h + 1) * LANE)
                right = slice(breadth + h * LANE, breadth + (h + 1) * LANE)
                stacked[k, top, left] = re
                stacked[k, top, right] = im
                stacked[k, low, left] = -im
                stacked[k, low, right] = re
        out = pltpu.make_async_copy(stacked.at[k], stacked_out.at[k], sem.at[2 + k])
        out.start()
        outs.append(out)
    for out in outs:
        out.wait()


def hand_on(scene_in, grad_in, scene_out, grad_out):
    scene_out[...] = scene_in[...]
    grad_out[...] = jnp.sum(grad_in[...], axis=0, keepdims=True)


def main_kernel(
    plan_ref,
    mask_in,
    trig_in,
    stacked_in,
    steer_in,
    scene_out,
    grad_ref,
    scene_ref,
    mask,
    omask,
    trig,
    stacked,
    steer,
    tiles,
    crecv,
    s1,
    r1a, r1b, r1c,
    s2a, s2b, s2c,
    r2a, r2b, r2c,
    s3a, s3b, s3c,
    r3a, r3b, r3c,
    units,
    wf,
    acc,
    lsem,
    msem,
    csend, crcv,
    s1send, s1recv,
    s2send, s2recv,
    s3send, s3recv,
    gsend, grecv,
    fsend, frecv,
):
    r1, s2, r2, s3, r3 = (r1a, r1b, r1c), (s2a, s2b, s2c), (r2a, r2b, r2c), (s3a, s3b, s3c), (r3a, r3b, r3c)
    where, core = position()
    y_own, z_own, x_own = turned(where, core)
    other = (y_own * 2 + 1 - core, z_own * SIDE + x_own)
    pulses = trig.shape[1]
    slots = steer.shape[0]

    for j in range(slots):
        pltpu.make_async_copy(steer_in.at[j], steer.at[j], lsem.at[j]).start()
    local = []
    for n, (src, dst) in enumerate(((mask_in, mask), (trig_in, trig), (stacked_in, stacked))):
        cp = pltpu.make_async_copy(src, dst, lsem.at[slots + n])
        cp.start()
        local.append(cp)

    barrier = pltpu.get_barrier_semaphore()
    pl.semaphore_signal(barrier, inc=1, device_id=other, device_id_type=MESH)
    for axis in range(3):
        for d in range(1, SIDE):
            pl.semaphore_signal(
                barrier, inc=1, device_id=device_at(shifted(where, axis, d), core), device_id_type=MESH
            )
    local[0].wait()
    local[1].wait()

    def turn(j, carry):
        pltpu.make_async_copy(steer_in.at[j], steer.at[j], lsem.at[j]).wait()
        cosine = trig[0:1, :]
        sines = trig[1:2, :]

        def rows(i, c2):
            at = pl.ds(pl.multiple_of(i * 64, 64), 64)
            re = steer[j, at, :pulses].astype(jnp.float32)
            im = steer[j, at, pulses:].astype(jnp.float32)
            steer[j, at, :pulses] = (re * cosine - im * sines).astype(jnp.bfloat16)
            steer[j, at, pulses:] = (re * sines + im * cosine).astype(jnp.bfloat16)
            return c2

        return lax.fori_loop(0, steer.shape[1] // 64, rows, carry)

    lax.fori_loop(0, slots, turn, 0)

    pl.semaphore_wait(barrier, 10)
    mcopy = pltpu.make_async_remote_copy(
        src_ref=mask, dst_ref=omask, send_sem=msem.at[0], recv_sem=msem.at[1], device_id=other, device_id_type=MESH
    )
    mcopy.start()
    local[2].wait()

    def core_copy(t):
        return pltpu.make_async_remote_copy(
            src_ref=tiles.at[t, :, 1 - core],
            dst_ref=crecv.at[t],
            send_sem=csend.at[0],
            recv_sem=crcv.at[t],
            device_id=other,
            device_id_type=MESH,
        )

    stage1, stage2, stage3 = {}, {}, {}

    def send1(p, d, src_fixed, key):
        lo, hi, order = PARTS[p]
        axis = order[0]
        fixed = dict(src_fixed)
        target = shifted(where, axis, d)
        fixed[axis] = target[axis]
        dst = tuple(src_fixed.get(a, slice(None)) for a in range(3) if a != axis)
        n = len(stage1)
        cp = pltpu.make_async_remote_copy(
            src_ref=s1.at[pick(fixed, lo, hi)],
            dst_ref=r1[p].at[(d - 1,) + dst],
            send_sem=s1send.at[0],
            recv_sem=s1recv.at[n],
            device_id=device_at(target, core),
            device_id_type=MESH,
        )
        cp.start()
        stage1[key] = cp

    def rest_index(p, fixed):
        return tuple(fixed.get(a, slice(None)) for a in range(3) if a != PARTS[p][2][0])

    def add_row(p, row):
        lo, hi, (a, b, c) = PARTS[p]

        def add(o, carry):
            here = rest_index(p, {b: row, c: o})
            v = s1[pick({a: where[a], b: row, c: o}, lo, hi)].astype(jnp.float32)
            for d in range(SIDE - 1):
                v = v + r1[p][(d,) + here].astype(jnp.float32)
            s2[p][here] = v.astype(jnp.bfloat16)
            return carry

        lax.fori_loop(0, SIDE, add, 0, unroll=True)

    def send2(p, d):
        b = PARTS[p][2][1]
        target = shifted(where, b, d)
        cp = pltpu.make_async_remote_copy(
            src_ref=s2[p].at[rest_index(p, {b: target[b]})],
            dst_ref=r2[p].at[d - 1],
            send_sem=s2send.at[0],
            recv_sem=s2recv.at[p * 3 + d - 1],
            device_id=device_at(target, core),
            device_id_type=MESH,
        )
        cp.start()
        stage2[p, d] = cp

    def row_done(p, g):
        for d in NEAR_FIRST:
            stage1[p, g, d].wait_recv()
        add_row(p, lax.rem(where[1] + 1 + g, SIDE))
        if g < SIDE - 1:
            send2(p, g + 1)

    def send3(p):
        lo, hi, (a, b, c) = PARTS[p]
        for d in NEAR_FIRST:
            stage2[p, d].wait_recv()
        for q in range(SIDE):
            v = s2[p][rest_index(p, {b: where[b], c: q})].astype(jnp.float32)
            for d in range(SIDE - 1):
                v = v + r2[p][d, q].astype(jnp.float32)
            s3[p][q] = v
        for d in NEAR_FIRST:
            target = shifted(where, c, d)
            cp = pltpu.make_async_remote_copy(
                src_ref=s3[p].at[target[c]],
                dst_ref=r3[p].at[d - 1],
                send_sem=s3send.at[p],
                recv_sem=s3recv.at[p * 3 + d - 1],
                device_id=device_at(target, core),
                device_id_type=MESH,
            )
            cp.start()
            stage3[p, d] = cp

    def column(i):
        return lax.rem(where[1] + 1 + i // SIDE, SIDE), i % SIDE

    def compute(i):
        z, x = column(i)
        t = z * SIDE + x
        left = steer[plan_ref[0, t]]
        right = stacked[plan_ref[1, t]]
        part = jnp.dot(left, right, preferred_element_type=jnp.float32)
        tiles[t] = part.reshape(tiles.shape[1:])
        core_copy(t).start()

    def combine(i):
        z, x = column(i)
        t = z * SIDE + x
        core_copy(t).wait_recv()
        for k in range(2):
            m = mask[pl.ds(t * 2 + k, 1), :]
            om = omask[pl.ds(t * 2 + k, 1), :]
            for lg in range(4):
                lanes = slice(lg * LANE, (lg + 1) * LANE)
                for y in range(SIDE):
                    v = tiles[t, y, core, :, lanes] * m + crecv[t, y, :, lanes] * om
                    u = k * 8 + lg * 2
                    s1[turned((y, z, x), core) + (slice(u, u + 2),)] = v.astype(jnp.bfloat16).reshape(2, SUB, LANE)

    def send_group(g):
        z = lax.rem(where[1] + 1 + g, SIDE)
        for d in NEAR_FIRST:
            send1(0, d, {1: z}, (0, g, d))
            send1(2, d, {1: z}, (2, g, d))
        if g < SIDE - 1:
            send1(1, g + 1, {}, (1, g + 1))

    def both(i, carry):
        compute(i)
        combine(i - LAG)
        return carry

    def first(i, carry):
        compute(i)
        return carry

    def final(i, carry):
        combine(i)
        return carry

    total = SIDE * SIDE
    lax.fori_loop(0, LAG, first, 0, unroll=2)
    mcopy.wait()
    lax.fori_loop(LAG, SIDE + LAG, both, 0, unroll=2)
    send_group(0)
    lax.fori_loop(SIDE + LAG, 2 * SIDE + LAG, both, 0, unroll=2)
    send_group(1)
    lax.fori_loop(2 * SIDE + LAG, 3 * SIDE + LAG, both, 0, unroll=2)
    send_group(2)
    lax.fori_loop(3 * SIDE + LAG, total, both, 0, unroll=2)
    lax.fori_loop(total - LAG, total, final, 0, unroll=2)
    send_group(3)

    for g in range(2):
        row_done(0, g)
        row_done(2, g)
    for d in NEAR_FIRST:
        stage1[1, d].wait_recv()
    for d in NEAR_FIRST:
        add_row(1, lax.rem(where[2] + d, SIDE))
        send2(1, d)
    add_row(1, where[2])
    row_done(0, 2)
    row_done(2, 2)
    send3(1)
    row_done(0, 3)
    send3(0)
    row_done(2, 3)
    send3(2)
    for p in (1, 0, 2):
        lo, hi, order = PARTS[p]
        v = s3[p][where[order[2]]]
        for d in range(1, SIDE):
            stage3[p, d].wait_recv()
            v = v + r3[p][d - 1]
        units[lo:hi] = v

    for k in range(2):
        for lg in range(2):
            for rh in range(2):
                ur = k * 8 + lg * 2 + rh
                re = units[ur]
                im = units[ur + 4]
                power = re * re + im * im
                wf[(core,) + where + (ur,)] = (re * power).astype(jnp.bfloat16)
                wf[(core,) + where + (ur + 4,)] = (im * power).astype(jnp.bfloat16)
                rows = slice(rh * SUB, (rh + 1) * SUB)
                scene_ref[k, rows, lg * LANE : (lg + 1) * LANE] = re
                scene_ref[k, rows, (lg + 2) * LANE : (lg + 3) * LANE] = im

    scene_copy = pltpu.make_async_copy(scene_ref, scene_out, lsem.at[0])
    scene_copy.start()

    gathers = {}

    def gather(p, fixed, axis, d, key, step):
        lo, hi, _ = GATHER_PARTS[p]
        src = wf.at[(core,) + pick(fixed, lo, hi)]
        n = len(gathers)
        cp = pltpu.make_async_remote_copy(
            src_ref=src,
            dst_ref=src,
            send_sem=gsend.at[step],
            recv_sem=grecv.at[n],
            device_id=device_at(shifted(where, axis, d), core),
            device_id_type=MESH,
        )
        cp.start()
        gathers[key] = cp

    def forward(p, fixed):
        lo, hi, _ = GATHER_PARTS[p]
        src = wf.at[(core,) + pick(fixed, lo, hi)]
        cp = pltpu.make_async_remote_copy(
            src_ref=src,
            dst_ref=src,
            send_sem=fsend.at[0],
            recv_sem=frecv.at[0],
            device_id=other,
            device_id_type=MESH,
        )
        cp.start()

    def back(axis, d):
        return lax.rem(where[axis] + SIDE - d, SIDE)

    order_of = (2, 0, 1)
    for p in order_of:
        for d in NEAR_FIRST:
            gather(p, dict(enumerate(where)), GATHER_PARTS[p][2][2], d, (p, "c", d), 0)

    def row_out(p, r):
        a, b, c = GATHER_PARTS[p][2]
        row = {a: where[a], b: back(b, r)}
        for d in NEAR_FIRST if r == LAST_ROW else (1, 3):
            gather(p, row, a, d, (p, r, d), 2)
        forward(p, row)

    for p in order_of:
        a, b, c = GATHER_PARTS[p][2]
        for d in NEAR_FIRST:
            gathers[p, "c", d].wait_recv()
        for d in NEAR_FIRST:
            gather(p, {a: where[a], b: where[b]}, b, d, (p, "b", d), 1)
        row_out(p, 0)
    def rows_on(d):
        for p in order_of:
            gathers[p, "b", d].wait_recv()
            row_out(p, d)

    def near_in(r):
        for p in order_of:
            a, b, c = GATHER_PARTS[p][2]
            for d, half in ((1, slice(0, 2)), (3, slice(2, 4))):
                gathers[p, r, d].wait_recv()
                gather(p, {a: back(a, d), b: back(b, r), c: half}, a, d, (p, r, "far", d), 2)
                forward(p, {a: back(a, d), b: back(b, r)})

    rows_on(1)
    rows_on(3)
    near_in(0)
    rows_on(2)
    near_in(1)
    near_in(3)
    for r in (0, 1, 3):
        for p in order_of:
            a, b, c = GATHER_PARTS[p][2]
            for d in (1, 3):
                gathers[p, r, "far", d].wait_recv()
            forward(p, {a: back(a, 2), b: back(b, r)})
    for d in NEAR_FIRST:
        for p in order_of:
            a, b, c = GATHER_PARTS[p][2]
            gathers[p, LAST_ROW, d].wait_recv()
            forward(p, {a: back(a, d), b: back(b, LAST_ROW)})
    pltpu.make_async_copy(wf.at[1 - core], wf.at[1 - core], frecv.at[0]).wait()

    acc[...] = jnp.zeros_like(acc)

    def backward(j, carry):
        zj = plan_ref[2, j]
        xj = plan_ref[3, j]
        kj = plan_ref[4, j]
        live = jnp.where(plan_ref[5, j] > 0, jnp.float32(1.0), jnp.float32(0.0))
        groups = []
        for lg in range(4):
            pieces = [
                wf[((c,) + ((y, zj, xj) if c == 0 else (xj, zj, y))) + (pl.ds(kj * 8 + lg * 2, 2),)].reshape(2 * SUB, LANE)
                for y in range(SIDE)
                for c in range(2)
            ]
            groups.append(jnp.concatenate(pieces, axis=0))
        weight = jnp.concatenate(groups, axis=1)
        moments = lax.dot_general(
            weight, stacked[kj], (((1,), (1,)), ((), ())), preferred_element_type=jnp.float32
        )
        re = steer[j, :, :pulses].astype(jnp.float32)
        im = steer[j, :, pulses:].astype(jnp.float32)
        term = im * moments[:, :pulses] - re * moments[:, pulses:]
        acc[...] += jnp.sum(term.reshape(-1, 8, pulses), axis=0) * live
        return carry

    lax.fori_loop(0, slots, backward, 0, unroll=4)
    factor = -4.0 / math.sqrt(steer.shape[1] * (stacked.shape[2] // 2))
    grad_ref[...] = acc[...] * factor

    scene_copy.wait()
    def all_sent(like, sem):
        pltpu.make_async_copy(like, like, sem).wait()

    all_sent(crecv, csend.at[0])
    all_sent(s1.at[:3], s1send.at[0])
    all_sent(s1.at[0, :3], s2send.at[0])
    for p in range(3):
        all_sent(r3[p], s3send.at[p])
    all_sent(wf.at[0, 0, 0, :3], gsend.at[0])
    all_sent(wf.at[0, 0, :3], gsend.at[1])
    all_sent(wf.at[0, :3], gsend.at[2])
    all_sent(wf.at[core], fsend.at[0])


def on_device(echoes, phases, kernel, steering, footprint, counts, range_start):
    columns = lax.axis_size("tile")
    row_parts = lax.axis_size("pulse")
    pulses = echoes.shape[0]
    breadth = kernel.shape[2]
    height = steering.shape[2]
    slots = steering.shape[1]
    tile_rows = range_start.shape[1]
    part_rows = height // row_parts
    width = 2 * breadth

    f32, bf16 = jnp.float32, jnp.bfloat16
    sizes = [hi - lo for lo, hi, _ in PARTS]
    vmem = pltpu.VMEM
    sem = lambda n: pltpu.SemaphoreType.DMA((n,))
    anywhere = pl.BlockSpec(memory_space=pl.ANY)
    smem = pl.BlockSpec(memory_space=pltpu.SMEM)
    whole = pl.BlockSpec(memory_space=pltpu.VMEM)
    span = kernel.shape[1] + LANE
    plan, mask, trig, stacked = pl.pallas_call(
        local_kernel,
        out_shape=(
            jax.ShapeDtypeStruct((6, columns), jnp.int32),
            jax.ShapeDtypeStruct((columns * tile_rows, LANE), f32),
            jax.ShapeDtypeStruct((2, pulses), f32),
            jax.ShapeDtypeStruct((tile_rows, 2 * pulses, width), bf16),
        ),
        in_specs=[smem] * 3 + [whole] * 2 + [anywhere],
        out_specs=[smem] + [whole] * 2 + [anywhere],
        scratch_shapes=[
            vmem((tile_rows, 2 * pulses, width), bf16),
            vmem((tile_rows, pulses, 2, span), bf16),
            vmem((SIDE, breadth // LANE, 2 * pulses // SIDE, LANE), f32),
            sem(4),
        ],
    )(footprint, counts, range_start, phases[None], kernel[0], echoes)
    scene, grad = pl.pallas_call(
        main_kernel,
        out_shape=(
            jax.ShapeDtypeStruct((tile_rows, part_rows, width), f32),
            jax.ShapeDtypeStruct((8, pulses), f32),
        ),
        in_specs=[smem] + [anywhere] * 4,
        out_specs=[anywhere, whole],
        scratch_shapes=[
            vmem((tile_rows, part_rows, width), f32),
            vmem((columns * tile_rows, LANE), f32),
            vmem((columns * tile_rows, LANE), f32),
            vmem((2, pulses), f32),
            vmem((tile_rows, 2 * pulses, width), bf16),
            vmem((slots, height, 2 * pulses), bf16),
            vmem((columns, SIDE, 2, part_rows, width), f32),
            vmem((columns, SIDE, part_rows, width), f32),
            vmem((SIDE, SIDE, SIDE, 16, SUB, LANE), bf16),
        ]
        + [vmem((3, SIDE, SIDE, n, SUB, LANE), bf16) for n in sizes]
        + [vmem((SIDE, SIDE, n, SUB, LANE), bf16) for n in sizes]
        + [vmem((3, SIDE, n, SUB, LANE), bf16) for n in sizes]
        + [vmem((SIDE, n, SUB, LANE), f32) for n in sizes]
        + [vmem((3, n, SUB, LANE), f32) for n in sizes]
        + [
            vmem((16, SUB, LANE), f32),
            vmem((2, SIDE, SIDE, SIDE, 16, SUB, LANE), bf16),
            vmem((8, pulses), f32),
            sem(slots + 3),
            sem(2),
            sem(1), sem(columns),
            sem(1), sem(27),
            sem(1), sem(9),
            sem(3), sem(9),
            sem(3), sem(66),
            sem(1), sem(1),
        ],
        compiler_params=pltpu.CompilerParams(
            collective_id=0, has_side_effects=True, vmem_limit_bytes=60 << 20
        ),
    )(plan, mask, trig, stacked, steering[0])
    scene, grad = pl.pallas_call(
        hand_on,
        out_shape=(
            jax.ShapeDtypeStruct(scene.shape, f32),
            jax.ShapeDtypeStruct((1, pulses), f32),
        ),
        in_specs=[whole] * 2,
        out_specs=[whole] * 2,
    )(scene, grad)
    return (scene[:, None], grad[0])


def solution(mesh):
    placed = (
        P(("pulse", "tile"), None, None),
        P(("pulse", "tile")),
        P(("pulse", "tile"), None, None),
        P(("pulse", "tile"), None, None, None),
        P(("pulse", "tile"), None),
        P(("pulse", "tile")),
        P(("pulse", "tile"), None),
    )
    return jax.shard_map(
        on_device,
        mesh=mesh,
        in_specs=placed,
        out_specs=(P(None, "tile", "pulse", None), P(("pulse", "tile"))),
        check_vma=False,
    )
```
